256 devices in a mesh: noise: 8 (over z), row: 16 (over y, x), col: 2 (over core).
Axes of the slice: x: 4, y: 4, z: 8, core: 2. Of those that a mesh axis runs over, the one named last changes fastest.
Arguments:
- images: bfloat16 [256, 4, 6144], P('row', None, 'col'), may hold values from -40 to 40
- gain: float32 [6144], P('col'), may hold values from 0.3 to 3.5
- up_weight: bfloat16 [6144, 12288], P('col', 'row'), may hold values from -0.078125 to 0.078125
- down_weight: bfloat16 [12288, 6144], P('row', 'col'), may hold values from -0.0546875 to 0.0546875
- cotangent: bfloat16 [256, 16, 6144], P('row', 'noise', 'col'), may hold values from -6 to 6
- seeds: int32 [16], P('noise'), may hold values from 0 to 999999
- assign: int32 [16, 1], replicated, may hold values from 0 to 3, as said below
Outputs:
- saliency: float32 [256, 4, 6144], P('row', None, 'col')
The draws below stay inside these ranges and needn't reach their ends.
Inputs may be any that keep to these rules, and one draw needn't show every extreme that they name: `assign`: every one of the 4 images is named by at least one copy.
All inputs are finite; a program needn't handle non-finite values.
Results may differ from the reference program's by a relative error of at most 0.0019.
Values may be sent and summed in bfloat16 or wider, within the bound.
A program may use at most 64 MiB of HBM per device.

```python
import math
import jax
import jax.numpy as jnp
from jax import lax

D = 6144
H = 12288
TOK_IMG = 256
SLOTS_ALL = 16
IMAGES = 4


def draw_images(key, part):
    key_feat, key_token, key_offset, key_base = jax.random.split(key, 4)
    position = jnp.arange(D, dtype=jnp.float32) / D
    feature = (0.5 + 1.5 * position) * jnp.exp(jax.random.uniform(key_feat, (D,), minval=-1.15, maxval=1.15))
    token = jnp.exp(jax.random.uniform(key_token, (TOK_IMG, IMAGES, 1), minval=-1.15, maxval=1.15))
    offset = jax.random.normal(key_offset, (TOK_IMG, IMAGES, 1), dtype=jnp.float32)
    base = jax.random.normal(key_base, (TOK_IMG, IMAGES, D), dtype=jnp.float32)
    values = token * feature * (base + offset)
    return jnp.clip(values, -40.0, 40.0).astype(jnp.bfloat16)


def draw_gain(key, part):
    position = jnp.arange(D, dtype=jnp.float32) / D
    factor = jnp.exp(jax.random.uniform(key, (D,), minval=-0.5, maxval=0.5))
    return ((0.5 + 1.5 * position) * factor).astype(jnp.float32)


def draw_assign(key, part):
    key_perm, key_rest = jax.random.split(jax.random.fold_in(key, 7))
    slot_index = jnp.arange(SLOTS_ALL, dtype=jnp.int32)
    rest = jax.random.randint(key_rest, (SLOTS_ALL,), 0, IMAGES, dtype=jnp.int32)
    base = jnp.where(slot_index < IMAGES, slot_index, rest)
    order = jax.random.permutation(key_perm, SLOTS_ALL)
    return base[order].astype(jnp.int32).reshape(SLOTS_ALL, 1)


def touch_ends(array, own_key, least, high):
    dims = array.shape
    spot = [jax.random.randint(jax.random.fold_in(own_key, axis), (), 0, dims[axis]) for axis in range(len(dims))]
    array = array.at[tuple(spot)].set(least)
    longest = dims.index(max(dims))
    spot[longest] = (spot[longest] + 1) % dims[longest]
    return array.at[tuple(spot)].set(high)


def steps_of(key, extent, cuts, least, largest):
    level = 1.0
    for dim, shards_of in cuts:
        heights = jax.random.uniform(jax.random.fold_in(jax.random.fold_in(key, 6), dim), (shards_of,), jnp.float32, least / len(cuts), largest / len(cuts))
        level = level * jnp.repeat(jnp.exp(heights), extent[dim] // shards_of).reshape((-1,) + (1,) * (len(extent) - 1 - dim))
    return level


def bell_draw(stream_key, dims, spread, limit, shards=(), held_as=jnp.bfloat16):
    array = spread * jax.random.normal(stream_key, dims, jnp.float32)
    if shards:
        array = array * steps_of(stream_key, dims, shards, -0.22, 0.18)
    return jnp.clip(array, -limit, limit).astype(held_as)


def setup_inputs(seed: int = 0) -> dict:
    key_list = jax.random.split(jax.random.key(seed), 8)
    images = draw_images(jax.random.fold_in(key_list[7], 71), 0)
    gain = draw_gain(jax.random.fold_in(key_list[7], 71), 0)
    up_weight = bell_draw(key_list[2], (D, H), D ** -0.5, 0.078125, ((0, 2), (1, 16)))
    down_weight = bell_draw(key_list[3], (H, D), H ** -0.5, 0.0546875, ((0, 16), (1, 2)))
    cotangent = bell_draw(key_list[4], (TOK_IMG, SLOTS_ALL, D), 1.0, 6.0, ((0, 16), (1, 8), (2, 2)))
    seeds = touch_ends(jax.random.randint(key_list[5], (SLOTS_ALL,), 0, 1000000), jax.random.fold_in(key_list[5], 1), 0, 999999).astype(jnp.int32)
    assign = draw_assign(jax.random.fold_in(key_list[7], 71), 0)
    return dict(images=images, gain=gain, up_weight=up_weight, down_weight=down_weight, cotangent=cotangent, seeds=seeds, assign=assign)


noise_scale = 0.6
gelu_coef = 0.044715
root_term = math.sqrt(2.0 / math.pi)

def mix_noise(seed_value, token_index, feature_index, width):
    linear = token_index[:, None] * width + feature_index[None, :]
    mixed = linear * 1664525 + seed_value * 1013904223
    mixed = mixed ^ mixed >> 13
    mixed = mixed * 1274126177
    mixed = mixed ^ mixed >> 16
    return ((mixed & 65535).astype(jnp.float32) - 32767.5) * (1.0 / 18918.0)

def gelu_slope(preact):
    inner = root_term * (preact + gelu_coef * preact * preact * preact)
    tanh_val = jnp.tanh(inner)
    return 0.5 * (1.0 + tanh_val) + 0.5 * preact * (1.0 - tanh_val * tanh_val) * root_term * (1.0 + 3.0 * gelu_coef * preact * preact)

def reference(images, gain, up_weight, down_weight, cotangent, seeds, assign):
    image_ids = jnp.arange(IMAGES, dtype=jnp.int32)
    onehot = (assign[:, 0][:, None] == image_ids[None, :]).astype(jnp.float32)
    clean_rows = jnp.einsum('si,tid->tsd', onehot, images.astype(jnp.float32), precision=lax.Precision.HIGHEST)
    token_index = jnp.arange(TOK_IMG, dtype=jnp.int32)
    feature_index = jnp.arange(D, dtype=jnp.int32)
    noise_field = jax.vmap(lambda seed_value: mix_noise(seed_value, token_index, feature_index, D), out_axes=1)(seeds)
    noisy_rows = clean_rows + noise_scale * noise_field
    feat_mean = lax.optimization_barrier(jnp.mean(noisy_rows, axis=-1, keepdims=True))
    centred = noisy_rows - feat_mean
    feat_var = lax.optimization_barrier(jnp.mean(centred * centred, axis=-1, keepdims=True))
    inv_std = lax.rsqrt(feat_var + 1e-06)
    normed = centred * inv_std
    scaled = (normed * gain).astype(jnp.bfloat16)
    row_count = TOK_IMG * seeds.shape[0]
    preact = jnp.dot(scaled.reshape(row_count, D), up_weight, preferred_element_type=jnp.float32)
    back_grad = jnp.dot(cotangent.reshape(row_count, D), down_weight.T, preferred_element_type=jnp.float32)
    hidden_grad = (back_grad * gelu_slope(preact)).astype(jnp.bfloat16)
    scaled_grad = jnp.dot(hidden_grad, up_weight.T, preferred_element_type=jnp.float32).reshape(cotangent.shape)
    normed_grad = scaled_grad * gain
    grad_sum = lax.optimization_barrier(jnp.mean(normed_grad, axis=-1, keepdims=True))
    grad_dot = lax.optimization_barrier(jnp.mean(normed_grad * normed, axis=-1, keepdims=True))
    input_grad = cotangent.astype(jnp.float32) + inv_std * (normed_grad - grad_sum - normed * grad_dot)
    totals = jnp.einsum('si,tsd->tid', onehot, input_grad, precision=lax.Precision.HIGHEST)
    counts = lax.optimization_barrier(jnp.sum(onehot, axis=0))
    return totals / counts[None, :, None]
```

```python
import math

import jax
import jax.numpy as jnp
from jax import lax
from jax.sharding import PartitionSpec as P

D = 6144

noise_scale = 0.6
gelu_coef = 0.044715
root_term = math.sqrt(2.0 / math.pi)


def mix_noise(seed_value, token_index, feature_index, width):
    linear = token_index[:, None] * width + feature_index[None, :]
    mixed = linear * 1664525 + seed_value * 1013904223
    mixed = mixed ^ mixed >> 13
    mixed = mixed * 1274126177
    mixed = mixed ^ mixed >> 16
    return ((mixed & 65535).astype(jnp.float32) - 32767.5) * (1.0 / 18918.0)


def gelu_slope(preact):
    inner = root_term * (preact + gelu_coef * preact * preact * preact)
    tanh_val = jnp.tanh(inner)
    return 0.5 * (1.0 + tanh_val) + 0.5 * preact * (1.0 - tanh_val * tanh_val) * root_term * (
        1.0 + 3.0 * gelu_coef * preact * preact
    )


def body(images, gain, up_weight, down_weight, cotangent, seeds, assign):
    tok_local = images.shape[0]
    image_count = images.shape[1]
    width_local = images.shape[2]
    planes = lax.axis_size("noise")
    rows = lax.axis_size("row")
    part = tok_local // planes
    col_index = lax.axis_index("col")
    row_index = lax.axis_index("row")
    noise_index = lax.axis_index("noise")
    all_seeds = lax.all_gather(seeds, "noise", tiled=True)
    slots = all_seeds.shape[0]
    own_cot = lax.all_to_all(cotangent, "noise", split_axis=0, concat_axis=1, tiled=True)
    own_images = lax.dynamic_slice_in_dim(images, noise_index * part, part)
    plane_images = lax.all_gather(own_images, "row", axis=0, tiled=True)
    plane_cot = lax.all_gather(own_cot, "row", axis=0, tiled=True)

    image_ids = jnp.arange(image_count, dtype=jnp.int32)
    onehot = (assign[:, 0][:, None] == image_ids[None, :]).astype(jnp.float32)
    counts = jnp.sum(onehot, axis=0)
    clean = jnp.einsum(
        "si,tid->tsd", onehot.astype(jnp.bfloat16), plane_images, preferred_element_type=jnp.float32
    )
    tokens = (
        jnp.arange(rows, dtype=jnp.int32)[:, None] * tok_local
        + noise_index * part
        + jnp.arange(part, dtype=jnp.int32)[None, :]
    ).reshape(-1)
    feature_index = col_index * width_local + jnp.arange(width_local, dtype=jnp.int32)
    noise_field = jax.vmap(
        lambda seed_value: mix_noise(seed_value, tokens, feature_index, D), out_axes=1
    )(all_seeds)
    noisy = clean + noise_scale * noise_field
    feat_mean = lax.psum(jnp.sum(noisy, axis=-1), "col") / D
    centred = noisy - feat_mean[..., None]
    feat_var = lax.psum(jnp.sum(centred * centred, axis=-1), "col") / D
    inv_std = lax.rsqrt(feat_var + 1e-06)
    normed = centred * inv_std[..., None]
    scaled = (normed * gain).astype(jnp.bfloat16)
    n = tokens.shape[0] * slots
    preact_part = jnp.dot(scaled.reshape(n, width_local), up_weight, preferred_element_type=jnp.float32)
    back_part = jnp.einsum(
        "td,hd->th", plane_cot.reshape(n, width_local), down_weight, preferred_element_type=jnp.float32
    )
    ug_part = jnp.sum(gain[:, None] * up_weight.astype(jnp.float32), axis=0)
    preact, back_grad, ug = lax.psum((preact_part, back_part, ug_part), "col")
    hidden_grad = (back_grad * gelu_slope(preact)).astype(jnp.bfloat16)
    hg = hidden_grad.astype(jnp.float32)
    sums = jnp.stack([jnp.sum(hg * ug, axis=-1), jnp.sum(hg * preact, axis=-1)], axis=-1) / D
    sums = lax.psum_scatter(sums.reshape(-1, slots, 2), "row", scatter_dimension=0, tiled=True)
    weighted = jnp.einsum(
        "ts,si,tsh->tih", inv_std, onehot, hg.reshape(-1, slots, hg.shape[-1]),
        precision=lax.Precision.HIGHEST,
    ).astype(jnp.bfloat16)
    grad = jnp.einsum(
        "th,dh->td", weighted.reshape(-1, hg.shape[-1]), up_weight, preferred_element_type=jnp.float32
    )
    grad = lax.psum_scatter(
        grad.reshape(-1, image_count, width_local), "row", scatter_dimension=0, tiled=True
    )
    own_normed = lax.dynamic_slice_in_dim(normed, row_index * part, part)
    own_inv = lax.dynamic_slice_in_dim(inv_std, row_index * part, part)
    rest = own_cot.astype(jnp.float32) - own_inv[..., None] * (
        sums[..., 0][..., None] + own_normed * sums[..., 1][..., None]
    )
    total = grad * gain + jnp.einsum("si,tsd->tid", onehot, rest, precision=lax.Precision.HIGHEST)
    total = total / counts[None, :, None]
    return lax.all_gather(total, "noise", axis=0, tiled=True)


def solution(mesh):
    placed = (
        P("row", None, "col"),
        P("col"),
        P("col", "row"),
        P("row", "col"),
        P("row", "noise", "col"),
        P("noise"),
        P(),
    )
    return jax.shard_map(
        body, mesh=mesh, in_specs=placed, out_specs=P("row", None, "col"), check_vma=False
    )
```

```python
import math

import jax
import jax.numpy as jnp
from jax import lax
from jax.experimental import pallas as pl
from jax.experimental.pallas import tpu as pltpu
from jax.sharding import PartitionSpec as P

D = 6144
NCH = 6
noise_scale = 0.6
gelu_coef = 0.044715
root_term = math.sqrt(2.0 / math.pi)
MESH = pl.DeviceIdType.MESH
F32 = jnp.float32
BF16 = jnp.bfloat16
I32 = jnp.int32


def gelu_slope(preact):
    inner = root_term * (preact + gelu_coef * preact * preact * preact)
    tanh_val = jnp.tanh(inner)
    return 0.5 * (1.0 + tanh_val) + 0.5 * preact * (1.0 - tanh_val * tanh_val) * root_term * (
        1.0 + 3.0 * gelu_coef * preact * preact
    )


def dot_nt(a, b):
    return lax.dot_general(a, b, (((1,), (1,)), ((), ())), preferred_element_type=F32)


def dot_nn(a, b):
    return lax.dot_general(a, b, (((1,), (0,)), ((), ())), preferred_element_type=F32)


def wrap(i, n):
    return lax.rem(i + n, n)


def kernel(
    img_hbm, gain_ref, up_hbm, dn_hbm, cot_hbm, seeds_ref, assign_ref, out_hbm,
    up_v, dn_v, img_own, pk16, imgg, rc, seedg, pk32, cg, onehot, base, noisy, scl,
    pre, pre_in, ugp, ug_in, slope, bk, bk_in, stat, stat_in, mi, gst, gst_in, wt, wm, wx, wx_in, wall,
    o_s, rs, rr1, ss, rr2, gx, gx_in, gy, gy_in, oh8, out_v,
    load_sem, z_send, z_recv, s_send, s_recv, i_send, i_recv, c_send, c_recv, k_send, k_recv,
    r_send, r_recv, g_send, g_recv, o_send, o_recv,
):
    W = 3072 // NCH
    z = lax.axis_index("noise")
    r = lax.axis_index("row")
    c = lax.axis_index("col")
    y, x = r // 4, lax.rem(r, 4)
    p1 = (x, y)
    p2 = (y, x)

    def row_peer(ab, phase, step):
        along_x = (ab == 0) == (phase == 1)
        if along_x:
            return {"row": y * 4 + wrap(x + step, 4)}
        return {"row": wrap(y + step, 4) * 4 + x}

    def z_peer(step):
        return {"noise": wrap(z + step, 8)}

    other = {"col": 1 - c}

    def rcopy(src, dst, ssem, rsem, dev):
        return pltpu.make_async_remote_copy(
            src_ref=src, dst_ref=dst, send_sem=ssem, recv_sem=rsem, device_id=dev, device_id_type=MESH
        )

    ld_img = pltpu.make_async_copy(img_hbm.at[pl.ds(2 * z, 2)], img_own, load_sem.at[0])
    ld_img.start()
    ld_cot = pltpu.make_async_copy(cot_hbm.at[pl.ds(2 * z, 2)], rc.at[z], load_sem.at[1])
    ld_cot.start()
    ld_up = pltpu.make_async_copy(up_hbm, up_v, load_sem.at[2])
    ld_up.start()
    ld_dn = pltpu.make_async_copy(dn_hbm, dn_v, load_sem.at[3])
    ld_dn.start()

    barrier = pltpu.get_barrier_semaphore()
    for dev in (
        [z_peer(s) for s in range(1, 8)]
        + [row_peer(0, 1, s) for s in (1, 2, 3)]
        + [row_peer(0, 2, s) for s in (1, 2, 3)]
        + [other]
    ):
        pl.semaphore_signal(barrier, inc=1, device_id=dev, device_id_type=MESH)

    seedg[z] = jnp.where(
        lax.broadcasted_iota(I32, (8, 128), 0) == 0, seeds_ref[0], seeds_ref[1]
    )
    ld_img.wait()
    for tok in range(2):
        v = img_own[tok].astype(F32)
        for q in range(4):
            ab, half = q // 2, q % 2
            pk16[half * 8 + tok * 4 : half * 8 + tok * 4 + 4, ab * 768 : (ab + 1) * 768] = v[
                :, q * 768 : (q + 1) * 768
            ]
    for ch in range(2):
        for ab in range(2):
            lo = ab * 768 + ch * 384
            imgg[ch, ab, p2[ab], p1[ab]] = pk16[:, lo : lo + 384].astype(BF16)
    pl.semaphore_wait(barrier, 14)

    sends = []
    z_order = (1, 7, 2, 6, 3, 5, 4)
    for s in z_order:
        peer = wrap(z + s, 8)
        cp = rcopy(cot_hbm.at[pl.ds(2 * peer, 2)], rc.at[z], z_send.at[s], z_recv.at[s], z_peer(s))
        cp.start()
        sends.append(cp)
        cp = rcopy(seedg.at[z], seedg.at[z], s_send.at[s], s_recv.at[s], z_peer(s))
        cp.start()
        sends.append(cp)

    class Gather:
        def __init__(self, buf, ssem, rsem, parity):
            self.buf, self.ssem, self.rsem, self.parity = buf, ssem, rsem, parity

        def blk(self, ab, a, b):
            return self.buf.at[ab, a, b]

        def ring(self, ab, phase):
            me = (p1 if phase == 1 else p2)[ab]

            def at(i):
                i = wrap(me + i, 4)
                return self.buf.at[ab, p2[ab], i] if phase == 1 else self.buf.at[ab, i]

            def mk(i, n, step):
                k = (ab * 2 + phase - 1) * 3 + n
                return rcopy(at(i), at(i), self.ssem.at[k], self.rsem.at[k], row_peer(ab, phase, step))

            right, left = mk(0, 0, 1), mk(0, 1, -1)
            fwd = mk(-1, 2, 1) if self.parity == 0 else mk(1, 2, -1)
            return right, left, fwd

        def first(self, phase):
            for ab in range(2):
                right, left, _ = self.ring(ab, phase)
                right.start()
                left.start()

        def second(self, phase):
            for ab in range(2):
                right, left, fwd = self.ring(ab, phase)
                right.wait_recv()
                left.wait_recv()
                fwd.start()

        def end(self, phase):
            for ab in range(2):
                self.ring(ab, phase)[2].wait_recv()

        def drain(self):
            for ab in range(2):
                for phase in (1, 2):
                    for cp in self.ring(ab, phase):
                        cp.wait_send()

    img_g = [Gather(imgg.at[ch], i_send.at[ch], i_recv.at[ch], ch) for ch in range(2)]
    cot_g = [Gather(cg.at[j], c_send.at[j], c_recv.at[j], j % 2) for j in range(NCH)]

    for g in img_g:
        g.first(1)

    sub16 = lax.broadcasted_iota(I32, (16, 128), 0)
    lane = lax.broadcasted_iota(I32, (16, 128), 1)
    a16 = jnp.zeros((16, 128), I32)
    for s in range(16):
        a16 = jnp.where(sub16 == s, assign_ref[s], a16)
    cnt = [jnp.float32(0.0)] * 4
    for s in range(16):
        for i in range(4):
            cnt[i] = cnt[i] + jnp.where(assign_ref[s] == i, 1.0, 0.0)
    sub8 = lax.broadcasted_iota(I32, (8, 128), 0)
    counts = jnp.zeros((8, 128), F32)
    for i in range(4):
        counts = jnp.where(lax.rem(sub8, 4) == i, cnt[i], counts)
    sel = jnp.zeros((8, 128), F32)
    lane8 = lax.broadcasted_iota(I32, (8, 128), 1)
    for tok in range(2):
        for s in range(16):
            hit = (lane8 == tok * 16 + s) & (sub8 == tok * 4 + assign_ref[s])
            sel = jnp.where(hit, 1.0, sel)
    oh8[...] = jnp.concatenate([sel, jnp.zeros((8, 128), F32)], axis=0).astype(BF16)

    def swap(b):
        return lax.rem(b, 4) * 4 + b // 4

    a16w = jnp.concatenate([a16, a16], axis=1)
    col16 = lax.broadcasted_iota(I32, (16, 256), 1)
    for tok in range(2):
        for ab in range(2):
            for half in range(2):

                def fill(b, _, tok=tok, ab=ab, half=half):
                    blk = b if tok == ab else swap(b)
                    target = a16w + (blk * 16 + half * 8 + tok * 4)
                    onehot[ab, half, pl.ds(pl.multiple_of(tok * 256 + b * 16, 16), 16), :] = jnp.where(
                        col16 == target, 1.0, 0.0
                    ).astype(BF16)
                    return 0

                lax.fori_loop(0, 16, fill, 0)

    for g in img_g:
        g.second(1)

    for s in z_order:
        peer = wrap(z - s, 8)
        rcopy(rc.at[peer], rc.at[peer], z_send.at[s], z_recv.at[s], z_peer(s)).wait_recv()
        rcopy(seedg.at[peer], seedg.at[peer], s_send.at[s], s_recv.at[s], z_peer(s)).wait_recv()
    ld_cot.wait()
    for k in range(8):
        for tok in range(2):
            pk32[tok * 16 + 2 * k : tok * 16 + 2 * k + 2, :] = rc[k, tok].astype(F32)
    for g in img_g:
        g.end(1)
        g.first(2)
    for j in range(NCH):
        for ab in range(2):
            cg[j, ab, p2[ab], p1[ab]] = pk32[ab * 16 : (ab + 1) * 16, j * W : (j + 1) * W].astype(BF16)
        cot_g[j].first(1)

    for k in range(8):
        for e in range(2):
            s = 2 * k + e
            pos = lax.broadcasted_iota(I32, (1, 3072), 1)
            row = seedg[k, e : e + 1, 0:1] * 1013904223
            base[s : s + 1, :] = (pos + c * 3072) * 1664525 + row

    g0 = gain_ref[...]
    g_hi = g0.astype(BF16)
    g_mid = (g0 - g_hi.astype(F32)).astype(BF16)
    g_lo = (g0 - g_hi.astype(F32) - g_mid.astype(F32)).astype(BF16)
    sub_g = lax.broadcasted_iota(I32, (16, 3072), 0)
    scl[512:528, :] = jnp.where(
        sub_g == 0,
        g_hi.astype(F32),
        jnp.where(sub_g == 1, g_mid.astype(F32), jnp.where(sub_g == 2, g_lo.astype(F32), 0.0)),
    ).astype(BF16)

    for g in img_g:
        g.second(2)
    cot_g[0].second(1)
    cot_g[1].second(1)
    cot_g[0].end(1)
    cot_g[0].first(2)
    for ch in range(2):
        img_g[ch].end(2)
        for ab in range(2):
            for half in range(2):
                lo = ab * 1536 + half * 768 + ch * 384
                noisy[:, lo : lo + 384] = dot_nn(onehot[ab, half], imgg[ch, ab].reshape(256, 384))

    def pump(k):
        if 0 <= k < NCH:
            cot_g[k].second(1)
        if 0 <= k - 1 < NCH:
            cot_g[k - 1].end(1)
            cot_g[k - 1].first(2)
        if 0 <= k - 2 < NCH:
            cot_g[k - 2].second(2)

    def token_of(tok, b):
        rr = b if tok == 0 else swap(b)
        return rr * 16 + z * 2 + tok

    def noise_block(tok, b, carry):
        tot, m2 = carry
        rows = pl.ds(pl.multiple_of(tok * 256 + b * 16, 16), 16)
        mixed = base[...] + token_of(tok, b) * D * 1664525
        mixed = mixed ^ (mixed >> 13)
        mixed = mixed * 1274126177
        mixed = mixed ^ (mixed >> 16)
        field = (mixed & 65535).astype(F32) - 32767.5
        v = noisy[rows, :] + field * (noise_scale / 18918.0)
        noisy[rows, :] = v
        s1 = jnp.sum(v, axis=1, keepdims=True)
        dev = v - s1 * (1.0 / 3072.0)
        s2 = jnp.sum(dev * dev, axis=1, keepdims=True)
        hit = lane == tok * 16 + b
        return jnp.where(hit, s1, tot), jnp.where(hit, s2, m2)

    carry = (jnp.zeros((16, 128), F32), jnp.zeros((16, 128), F32))
    carry = lax.fori_loop(0, 8, lambda b, cr: noise_block(0, b, cr), carry)
    pump(2)
    carry = lax.fori_loop(8, 16, lambda b, cr: noise_block(0, b, cr), carry)
    carry = lax.fori_loop(0, 8, lambda b, cr: noise_block(1, b, cr), carry)
    pump(3)
    carry = lax.fori_loop(8, 16, lambda b, cr: noise_block(1, b, cr), carry)
    stat[0], stat[1] = carry
    cp_stat = rcopy(stat, stat_in, k_send.at[0], k_recv.at[0], other)
    cp_stat.start()
    pump(4)
    cp_stat.wait_recv()
    mean_a, mean_b = stat[0] * (1.0 / 3072.0), stat_in[0] * (1.0 / 3072.0)
    gap = mean_a - mean_b
    var = (stat[1] + stat_in[1] + gap * gap * 1536.0) * (1.0 / D)
    mi[0] = (mean_a + mean_b) * 0.5
    mi[1] = lax.rsqrt(var + 1e-06)

    def pick(arr, idx):
        return jnp.sum(jnp.where(lane == idx, arr, 0.0), axis=1, keepdims=True)

    def norm_block(k, _):
        rows = pl.ds(pl.multiple_of(k * 16, 16), 16)
        normed = (noisy[rows, :] - pick(mi[0], k)) * pick(mi[1], k)
        scl[rows, :] = (normed * gain_ref[...]).astype(BF16)
        return 0

    lax.fori_loop(0, 32, norm_block, 0)
    pump(5)
    ld_up.wait()
    ld_dn.wait()

    def pre_cols(n):
        res = dot_nn(scl[...], up_v[:, n * 256 : (n + 1) * 256])
        pre[0, :, n * 256 : (n + 1) * 256] = res[0:256]
        pre[1, :, n * 256 : (n + 1) * 256] = res[256:512]
        ugp[:, n * 256 : (n + 1) * 256] = res[512:528]

    pre_cols(0)
    pump(6)
    pre_cols(1)
    pump(7)
    pre_cols(2)
    cp_pre = rcopy(pre.at[1 - c], pre_in, k_send.at[1], k_recv.at[1], other)
    cp_pre.start()
    cp_ug = rcopy(ugp, ug_in, k_send.at[2], k_recv.at[2], other)
    cp_ug.start()

    def back_chunk(j, ab):
        dim = cg[j, ab].reshape(256, W)
        res = dot_nt(dim, dn_v[:, j * W : (j + 1) * W])
        if j == 0:
            bk[ab] = res
        else:
            bk[ab] = bk[ab] + res

    for j in range(NCH - 1):
        cot_g[j].end(2)
        for ab in range(2):
            back_chunk(j, ab)
        if j == 0:
            cp_pre.wait_recv()
            cp_ug.wait_recv()
        if j == 1:

            def slope_block(k, _):
                rows = pl.ds(pl.multiple_of(k * 16, 16), 16)
                p = pre[c, rows, :] + pre_in[rows, :]
                pre_in[rows, :] = p
                slope[rows, :] = gelu_slope(p)
                return 0

            lax.fori_loop(0, 16, slope_block, 0)
        if j == 2:
            def wt_block(b, _):
                rr = jnp.where(c == 0, b, swap(b))
                inv = pick(mi[1], c * 16 + b)
                wt[pl.ds(pl.multiple_of(b * 16, 16), 16), :] = jnp.where(
                    lane == rr * 8 + c * 4 + a16, inv, 0.0
                )
                return 0

            lax.fori_loop(0, 16, wt_block, 0)
            full = wt[...].T
            hi = full.astype(BF16)
            mid = (full - hi.astype(F32)).astype(BF16)
            lo = (full - hi.astype(F32) - mid.astype(F32)).astype(BF16)
            wm[0:128] = hi
            wm[128:256] = mid
            wm[256:384] = lo
    cot_g[NCH - 1].end(2)
    last = NCH - 1
    for flip in (1, 0):
        ab = (c + flip) % 2
        dim = cg[last, ab].reshape(256, W)
        bk[ab] = bk[ab] + dot_nt(dim, dn_v[:, last * W :])
        if flip == 1:
            cp_bk = rcopy(bk.at[1 - c], bk_in, k_send.at[3], k_recv.at[3], other)
            cp_bk.start()
    ug = (ugp[0:1] + ugp[1:2] + ugp[2:3]) + (ug_in[0:1] + ug_in[1:2] + ug_in[2:3])
    cp_bk.wait_recv()

    def hidden_block(b, carry):
        gs, gd = carry
        rows = pl.ds(pl.multiple_of(b * 16, 16), 16)
        hg = ((bk[c, rows, :] + bk_in[rows, :]) * slope[rows, :]).astype(BF16)
        scl[rows, 0:768] = hg
        hf = hg.astype(F32)
        s1 = jnp.sum(hf * ug, axis=1, keepdims=True)
        s2 = jnp.sum(hf * pre_in[rows, :], axis=1, keepdims=True)
        hit = lane == c * 16 + b
        return jnp.where(hit, s1, gs), jnp.where(hit, s2, gd)

    zero = jnp.zeros((16, 128), F32)
    gst[0], gst[1] = lax.fori_loop(0, 16, hidden_block, (zero, zero))
    cp_gst = rcopy(gst, gst_in, k_send.at[4], k_recv.at[4], other)
    cp_gst.start()
    wsum = dot_nn(wm[...], scl[0:256, 0:768])
    wsum = wsum[0:128] + wsum[128:256] + wsum[256:384]
    w_hi = wsum.astype(BF16)
    wx[0:128] = w_hi
    wx[128:256] = (wsum - w_hi.astype(F32)).astype(BF16)
    cp_wx = rcopy(wx, wx_in, k_send.at[5], k_recv.at[5], other)
    cp_wx.start()

    cp_gst.wait_recv()
    gx[...] = gst[...] + gst_in[...]

    def g_copy(axis, src, dst, step):
        k = axis * 3 + step - 1
        return rcopy(src, dst.at[step - 1], g_send.at[k], g_recv.at[k], row_peer(0, axis + 1, step))

    for step in (1, 2, 3):
        g_copy(0, gx, gx_in, step).start()

    cp_wx.wait_recv()
    wall[...] = (wx[...].astype(F32) + wx_in[...].astype(F32)).astype(BF16)

    def r1_copy(ab, step):
        k = ab * 6 + step - 1
        return rcopy(
            rs.at[ab, wrap(p1[ab] + step, 4)], rr1.at[ab, step - 1], r_send.at[k], r_recv.at[k], row_peer(ab, 1, step)
        )

    def r2_copy(ab, step):
        k = ab * 6 + 3 + step - 1
        return rcopy(
            ss.at[ab, wrap(p2[ab] + step, 4)], rr2.at[ab, step - 1], r_send.at[k], r_recv.at[k], row_peer(ab, 2, step)
        )

    for ab in range(2):
        for half in range(2):
            q = ab * 2 + half
            o = dot_nt(wall[...], up_v[q * 768 : (q + 1) * 768, :])
            o_s[ab, half] = o[0:128] + o[128:256]

        def pack(k, _, ab=ab):
            rows = pl.ds(pl.multiple_of(k * 8, 8), 8)
            both = jnp.concatenate([o_s[ab, 0, rows, :], o_s[ab, 1, rows, :]], axis=0)
            ky, kx = k // 4, lax.rem(k, 4)
            rs[ab, kx if ab == 0 else ky, ky if ab == 0 else kx] = both.astype(BF16)
            return 0

        lax.fori_loop(0, 16, pack, 0)
        for step in (1, 2, 3):
            r1_copy(ab, step).start()
        if ab == 0:
            for step in (1, 2, 3):
                g_copy(0, gx, gx_in, step).wait_recv()
            gy[...] = gx[...] + gx_in[0] + gx_in[1] + gx_in[2]
            for step in (1, 2, 3):
                g_copy(1, gy, gy_in, step).start()

    for step in (1, 2, 3):
        g_copy(1, gy, gy_in, step).wait_recv()
    gtot = (gy[...] + gy_in[0] + gy_in[1] + gy_in[2]) * (1.0 / D)
    own_b = (y * 4 + x, x * 4 + y)
    for tok in range(2):
        k = tok * 16 + own_b[tok]
        rows = pl.ds(pl.multiple_of(tok * 256 + own_b[tok] * 16, 16), 16)
        inv = pick(mi[1], k)
        normed = (noisy[rows, :] - pick(mi[0], k)) * inv
        v = inv * (pick(gtot[0], k) + normed * pick(gtot[1], k))
        pk32[tok * 16 : tok * 16 + 16, :] = pk32[tok * 16 : tok * 16 + 16, :] - v
    rest = pk32[...]
    t1 = rest.astype(BF16)
    t2 = (rest - t1.astype(F32)).astype(BF16)
    t3 = (rest - t1.astype(F32) - t2.astype(F32)).astype(BF16)
    pick8 = oh8[:, 0:32]
    rest8 = (dot_nn(pick8, t1) + dot_nn(pick8, t2) + dot_nn(pick8, t3))[0:8]

    for ab in range(2):
        for step in (1, 2, 3):
            r1_copy(ab, 4 - step).wait_recv()

        def add1(k, _, ab=ab):
            kr = (k * 4 + p1[0]) if ab == 0 else (p1[1] * 4 + k)
            rows = pl.ds(pl.multiple_of(kr * 8, 8), 8)
            both = jnp.concatenate([o_s[ab, 0, rows, :], o_s[ab, 1, rows, :]], axis=0)
            for n in range(3):
                both = both + rr1[ab, n, k].astype(F32)
            ss[ab, k] = both.astype(BF16)
            return 0

        lax.fori_loop(0, 4, add1, 0)
        for step in (1, 2, 3):
            r2_copy(ab, step).start()

    cnt8 = counts[:, 0:1]
    for ab in range(2):
        for step in (1, 2, 3):
            r2_copy(ab, step).wait_recv()
        tot = ss[ab, p2[ab]].astype(F32)
        for n in range(3):
            tot = tot + rr2[ab, n].astype(F32)
        for half in range(2):
            lo = ab * 1536 + half * 768
            g8 = tot[half * 8 : half * 8 + 8] * gain_ref[:, lo : lo + 768]
            fin = (g8 + rest8[:, lo : lo + 768]) / cnt8
            out_v[2 * z, :, lo : lo + 768] = fin[0:4]
            out_v[2 * z + 1, :, lo : lo + 768] = fin[4:8]

    def o_copy(n, way):
        step = 1 if way == 0 else -1
        src = wrap(z - step * (n - 1) + 8, 8)
        k = (n - 1) * 2 + way
        if n < 4:
            ref = out_v.at[pl.ds(2 * src, 2)]
        else:
            ref = out_v.at[pl.ds(2 * src + way, 1)]
        return rcopy(ref, ref, o_send.at[k], o_recv.at[k], z_peer(step))

    for n in (1, 2, 3, 4):
        for way in (0, 1):
            if n > 1:
                o_copy(n - 1, way).wait_recv()
            o_copy(n, way).start()
    for way in (0, 1):
        o_copy(4, way).wait_recv()
    st_out = pltpu.make_async_copy(out_v, out_hbm, load_sem.at[4])
    st_out.start()
    for cp in sends:
        cp.wait_send()
    for g in img_g + cot_g:
        g.drain()
    for cp in (cp_stat, cp_pre, cp_ug, cp_bk, cp_gst, cp_wx):
        cp.wait_send()
    for axis in range(2):
        for step in (1, 2, 3):
            g_copy(axis, gx, gx_in, step).wait_send()
    for ab in range(2):
        for step in (1, 2, 3):
            r1_copy(ab, step).wait_send()
            r2_copy(ab, step).wait_send()
    for n in (1, 2, 3, 4):
        for way in (0, 1):
            o_copy(n, way).wait_send()
    st_out.wait()


def body(images, gain, up_weight, down_weight, cotangent, seeds, assign):
    W = 3072 // NCH
    vm, dma = pltpu.VMEM, pltpu.SemaphoreType.DMA
    anyspace = pl.BlockSpec(memory_space=pl.ANY)
    return pl.pallas_call(
        kernel,
        out_shape=jax.ShapeDtypeStruct((16, 4, 3072), F32),
        in_specs=[
            anyspace,
            pl.BlockSpec(memory_space=pltpu.VMEM),
            anyspace,
            anyspace,
            anyspace,
            pl.BlockSpec(memory_space=pltpu.SMEM),
            pl.BlockSpec(memory_space=pltpu.SMEM),
        ],
        out_specs=anyspace,
        scratch_shapes=[
            vm((3072, 768), BF16),
            vm((768, 3072), BF16),
            vm((2, 4, 3072), BF16),
            vm((16, 1536), F32),
            vm((2, 2, 4, 4, 16, 384), BF16),
            vm((8, 2, 2, 3072), BF16),
            vm((8, 8, 128), I32),
            vm((32, 3072), F32),
            vm((NCH, 2, 4, 4, 16, W), BF16),
            vm((2, 2, 512, 256), BF16),
            vm((16, 3072), I32),
            vm((512, 3072), F32),
            vm((528, 3072), BF16),
            vm((2, 256, 768), F32),
            vm((256, 768), F32),
            vm((16, 768), F32),
            vm((16, 768), F32),
            vm((256, 768), F32),
            vm((2, 256, 768), F32),
            vm((256, 768), F32),
            vm((2, 16, 128), F32),
            vm((2, 16, 128), F32),
            vm((2, 16, 128), F32),
            vm((2, 16, 128), F32),
            vm((2, 16, 128), F32),
            vm((256, 128), F32),
            vm((384, 256), BF16),
            vm((256, 768), BF16),
            vm((256, 768), BF16),
            vm((256, 768), BF16),
            vm((2, 2, 128, 768), F32),
            vm((2, 4, 4, 16, 768), BF16),
            vm((2, 3, 4, 16, 768), BF16),
            vm((2, 4, 16, 768), BF16),
            vm((2, 3, 16, 768), BF16),
            vm((2, 16, 128), F32),
            vm((3, 2, 16, 128), F32),
            vm((2, 16, 128), F32),
            vm((3, 2, 16, 128), F32),
            vm((16, 128), BF16),
            vm((16, 4, 3072), F32),
            dma((5,)),
            dma((8,)), dma((8,)),
            dma((8,)), dma((8,)),
            dma((2, 12)), dma((2, 12)),
            dma((NCH, 12)), dma((NCH, 12)),
            dma((6,)), dma((6,)),
            dma((12,)), dma((12,)),
            dma((6,)), dma((6,)),
            dma((8,)), dma((8,)),
        ],
        compiler_params=pltpu.CompilerParams(
            collective_id=0, has_side_effects=True, vmem_limit_bytes=56 * 1024 * 1024
        ),
        cost_estimate=pl.CostEstimate(flops=8 * 10**9, bytes_accessed=12 * 10**6, transcendentals=200000),
    )(images, gain.reshape(1, -1), up_weight, down_weight, cotangent, seeds, assign.reshape(-1))


def solution(mesh):
    placed = (
        P("row", None, "col"),
        P("col"),
        P("col", "row"),
        P("row", "col"),
        P("row", "noise", "col"),
        P("noise"),
        P(),
    )
    return jax.shard_map(
        body, mesh=mesh, in_specs=placed, out_specs=P("row", None, "col"), check_vma=False
    )
```

```python
import functools
import math

import jax
import jax.numpy as jnp
from jax import lax
from jax.experimental import pallas as pl
from jax.experimental.pallas import tpu as pltpu
from jax.sharding import PartitionSpec as P

D = 6144
NCH = 4
noise_scale = 0.6
gelu_coef = 0.044715
root_term = math.sqrt(2.0 / math.pi)
MESH = pl.DeviceIdType.MESH
F32 = jnp.float32
BF16 = jnp.bfloat16
I32 = jnp.int32


def gelu_slope(preact):
    inner = root_term * (preact + gelu_coef * preact * preact * preact)
    tanh_val = jnp.tanh(inner)
    return 0.5 * (1.0 + tanh_val) + 0.5 * preact * (1.0 - tanh_val * tanh_val) * root_term * (
        1.0 + 3.0 * gelu_coef * preact * preact
    )


def dot_nt(a, b):
    return lax.dot_general(a, b, (((1,), (1,)), ((), ())), preferred_element_type=F32)


def dot_nn(a, b):
    return lax.dot_general(a, b, (((1,), (0,)), ((), ())), preferred_element_type=F32)


class Copy:
    def __init__(self, live, src, dst, ssem, rsem, dev):
        self.live, self.got = live, False
        self.make = lambda: pltpu.make_async_remote_copy(
            src_ref=src, dst_ref=dst, send_sem=ssem, recv_sem=rsem, device_id=dev, device_id_type=MESH
        )

    def start(self):
        self.made = self.make()
        self.made.start()
        self.live.append(self)

    def wait_recv(self):
        self.made.wait_recv()
        self.got = True

    def wait_send(self):
        self.made.wait_send()


def wrap(i, n):
    return lax.rem(i + n, n)


def kernel(
    img_hbm, gain_ref, up_hbm, dn_hbm, cot_hbm, seeds_ref, assign_ref, outa_hbm, outb_hbm,
    up_v, dn_v, img_own, pk16, imgg, rc, seedg, pk32, cg, onehot, base, noisy, scl,
    pre, pre_in, ugp, ug_in, slope, bk, bk_in, stat, stat_in, mi, gst, gst_in, wt, wm, wx, wx_in, wall,
    o_s, rs, rr, gx, gx_in, gy, gy_in, oh8, ea_own, la_own,
    load_sem, z_send, z_recv, s_send, s_recv, i_send, i_recv, c_send, c_recv, k_send, k_recv,
    r_send, r_recv, g_send, g_recv, e_send, e_recv, l_send, l_recv,
):
    W = 3072 // NCH
    z = lax.axis_index("noise")
    r = lax.axis_index("row")
    c = lax.axis_index("col")
    y, x = r // 4, lax.rem(r, 4)
    p1 = (x, y)
    p2 = (y, x)

    def row_peer(ab, phase, step):
        along_x = (ab == 0) == (phase == 1)
        if along_x:
            return {"row": y * 4 + wrap(x + step, 4)}
        return {"row": wrap(y + step, 4) * 4 + x}

    def z_peer(step):
        return {"noise": wrap(z + step, 8)}

    other = {"col": 1 - c}

    live = []

    def rcopy(src, dst, ssem, rsem, dev):
        return Copy(live, src, dst, ssem, rsem, dev)

    ld_img = pltpu.make_async_copy(img_hbm.at[pl.ds(2 * z, 2)], img_own, load_sem.at[0])
    ld_img.start()
    ld_cot = pltpu.make_async_copy(cot_hbm.at[pl.ds(2 * z, 2)], rc.at[z], load_sem.at[1])
    ld_cot.start()
    ld_up = pltpu.make_async_copy(up_hbm, up_v, load_sem.at[2])
    ld_up.start()
    ld_dn = pltpu.make_async_copy(dn_hbm, dn_v, load_sem.at[3])
    ld_dn.start()

    barrier = pltpu.get_barrier_semaphore()
    for dev in (
        [z_peer(s) for s in range(1, 8)]
        + [{"row": wrap(y + k // 4, 4) * 4 + wrap(x + k % 4, 4)} for k in range(1, 16)]
        + [other]
    ):
        pl.semaphore_signal(barrier, inc=1, device_id=dev, device_id_type=MESH)

    seedg[z] = jnp.where(
        lax.broadcasted_iota(I32, (8, 128), 0) == 0, seeds_ref[0], seeds_ref[1]
    )
    ld_img.wait()
    for tok in range(2):
        v = img_own[tok].astype(F32)
        for q in range(4):
            ab, half = q // 2, q % 2
            pk16[half * 8 + tok * 4 : half * 8 + tok * 4 + 4, ab * 768 : (ab + 1) * 768] = v[
                :, q * 768 : (q + 1) * 768
            ]
    for ch in range(2):
        for ab in range(2):
            lo = ab * 768 + ch * 384
            imgg[ch, ab, p2[ab], p1[ab]] = pk16[:, lo : lo + 384].astype(BF16)
    pl.semaphore_wait(barrier, 23)

    z_order = (1, 7, 2, 6, 3, 5, 4)
    z_cot, z_seed = {}, {}
    for s in z_order:
        peer = wrap(z + s, 8)
        z_cot[s] = rcopy(cot_hbm.at[pl.ds(2 * peer, 2)], rc.at[z], z_send.at[s], z_recv.at[s], z_peer(s))
        z_seed[s] = rcopy(seedg.at[z], seedg.at[z], s_send.at[s], s_recv.at[s], z_peer(s))
        z_cot[s].start()
        z_seed[s].start()

    class Gather:
        def __init__(self, buf, ssem, rsem):
            self.copies = {}
            for ab in range(2):
                for phase in (1, 2):
                    own = buf.at[ab, p2[ab], p1[ab]] if phase == 1 else buf.at[ab, p2[ab]]
                    for step in (1, 3, 2):
                        k = (ab * 2 + phase - 1) * 3 + step - 1
                        self.copies[ab, phase, step] = rcopy(
                            own, own, ssem.at[k], rsem.at[k], row_peer(ab, phase, step)
                        )

        def start(self, phase):
            for step in (1, 3, 2):
                for ab in range(2):
                    self.copies[ab, phase, step].start()

        def wait(self, phase):
            for step in (1, 3, 2):
                for ab in range(2):
                    self.copies[ab, phase, step].wait_recv()

    img_g = [Gather(imgg.at[ch], i_send.at[ch], i_recv.at[ch]) for ch in range(2)]
    cot_g = [Gather(cg.at[j], c_send.at[j], c_recv.at[j]) for j in range(NCH)]

    for g in img_g:
        g.start(1)

    sub16 = lax.broadcasted_iota(I32, (16, 128), 0)
    lane = lax.broadcasted_iota(I32, (16, 128), 1)
    a16 = jnp.zeros((16, 128), I32)
    for s in range(16):
        a16 = jnp.where(sub16 == s, assign_ref[s], a16)
    cnt = [jnp.float32(0.0)] * 4
    for s in range(16):
        for i in range(4):
            cnt[i] = cnt[i] + jnp.where(assign_ref[s] == i, 1.0, 0.0)
    sub8 = lax.broadcasted_iota(I32, (8, 128), 0)
    counts = jnp.zeros((8, 128), F32)
    for i in range(4):
        counts = jnp.where(lax.rem(sub8, 4) == i, cnt[i], counts)
    cnt8 = counts[:, 0:1]
    sel = jnp.zeros((8, 128), F32)
    lane8 = lax.broadcasted_iota(I32, (8, 128), 1)
    for tok in range(2):
        for s in range(16):
            hit = (lane8 == tok * 16 + s) & (sub8 == tok * 4 + assign_ref[s])
            sel = jnp.where(hit, 1.0, sel)
    oh8[...] = jnp.concatenate([sel, jnp.zeros((8, 128), F32)], axis=0).astype(BF16)

    def swap(b):
        return lax.rem(b, 4) * 4 + b // 4

    a16w = jnp.concatenate([a16, a16], axis=1)
    col16 = lax.broadcasted_iota(I32, (16, 256), 1)
    for tok in range(2):
        for ab in range(2):
            for half in range(2):

                def fill(b, _, tok=tok, ab=ab, half=half):
                    blk = b if tok == ab else swap(b)
                    target = a16w + (blk * 16 + half * 8 + tok * 4)
                    onehot[ab, half, pl.ds(pl.multiple_of(tok * 256 + b * 16, 16), 16), :] = jnp.where(
                        col16 == target, 1.0, 0.0
                    ).astype(BF16)
                    return 0

                lax.fori_loop(0, 16, fill, 0)

    for g in img_g:
        g.wait(1)
        g.start(2)

    for s in z_order:
        z_cot[s].wait_recv()
        z_seed[s].wait_recv()
    ld_cot.wait()
    for k in range(8):
        for tok in range(2):
            pk32[tok * 16 + 2 * k : tok * 16 + 2 * k + 2, :] = rc[k, tok].astype(F32)
    for j in range(NCH):
        for ab in range(2):
            cg[j, ab, p2[ab], p1[ab]] = pk32[ab * 16 : (ab + 1) * 16, j * W : (j + 1) * W].astype(BF16)
        cot_g[j].start(1)
    early8 = dot_nn(oh8[:, 0:32], pk32[...].astype(BF16))[0:8] / cnt8
    ea_own[0], ea_own[1] = early8[0:4], early8[4:8]
    ld_ea = pltpu.make_async_copy(ea_own, outa_hbm.at[pl.ds(2 * z, 2)], load_sem.at[4])
    ld_ea.start()
    ea = {s: rcopy(ea_own, outa_hbm.at[pl.ds(2 * z, 2)], e_send.at[s], e_recv.at[s], z_peer(s)) for s in z_order}
    for s in z_order:
        ea[s].start()

    for k in range(8):
        for e in range(2):
            s = 2 * k + e
            pos = lax.broadcasted_iota(I32, (1, 3072), 1)
            row = seedg[k, e : e + 1, 0:1] * 1013904223
            base[s : s + 1, :] = (pos + c * 3072) * 1664525 + row

    g0 = gain_ref[...]
    g_hi = g0.astype(BF16)
    g_mid = (g0 - g_hi.astype(F32)).astype(BF16)
    g_lo = (g0 - g_hi.astype(F32) - g_mid.astype(F32)).astype(BF16)
    sub_g = lax.broadcasted_iota(I32, (16, 3072), 0)
    scl[512:528, :] = jnp.where(
        sub_g == 0,
        g_hi.astype(F32),
        jnp.where(sub_g == 1, g_mid.astype(F32), jnp.where(sub_g == 2, g_lo.astype(F32), 0.0)),
    ).astype(BF16)

    for ch in range(2):
        img_g[ch].wait(2)
        for ab in range(2):
            for half in range(2):
                lo = ab * 1536 + half * 768 + ch * 384
                noisy[:, lo : lo + 384] = dot_nn(onehot[ab, half], imgg[ch, ab].reshape(256, 384))

    def pump(k):
        cot_g[k].wait(1)
        cot_g[k].start(2)

    pump(0)

    def token_of(tok, b):
        rr = b if tok == 0 else swap(b)
        return rr * 16 + z * 2 + tok

    def noise_block(tok, b, carry):
        tot, m2 = carry
        rows = pl.ds(pl.multiple_of(tok * 256 + b * 16, 16), 16)
        mixed = base[...] + token_of(tok, b) * D * 1664525
        mixed = mixed ^ (mixed >> 13)
        mixed = mixed * 1274126177
        mixed = mixed ^ (mixed >> 16)
        field = (mixed & 65535).astype(F32) - 32767.5
        v = noisy[rows, :] + field * (noise_scale / 18918.0)
        noisy[rows, :] = v
        s1 = jnp.sum(v, axis=1, keepdims=True)
        dev = v - s1 * (1.0 / 3072.0)
        s2 = jnp.sum(dev * dev, axis=1, keepdims=True)
        hit = lane == tok * 16 + b
        return jnp.where(hit, s1, tot), jnp.where(hit, s2, m2)

    carry = (jnp.zeros((16, 128), F32), jnp.zeros((16, 128), F32))
    def noise_blocks(tok, first, carry):
        def four(k, cr):
            for u in range(4):
                cr = noise_block(tok, first + k * 4 + u, cr)
            return cr

        return lax.fori_loop(0, 2, four, carry)

    carry = noise_blocks(0, 0, carry)
    pump(1)
    carry = noise_blocks(0, 8, carry)
    pump(2)
    carry = noise_blocks(1, 0, carry)
    pump(3)
    carry = noise_blocks(1, 8, carry)
    stat[0], stat[1] = carry
    cp_stat = rcopy(stat, stat_in, k_send.at[0], k_recv.at[0], other)
    cp_stat.start()
    cp_stat.wait_recv()
    mean_a, mean_b = stat[0] * (1.0 / 3072.0), stat_in[0] * (1.0 / 3072.0)
    gap = mean_a - mean_b
    var = (stat[1] + stat_in[1] + gap * gap * 1536.0) * (1.0 / D)
    mi[0] = (mean_a + mean_b) * 0.5
    mi[1] = lax.rsqrt(var + 1e-06)

    def pick(arr, idx):
        return jnp.sum(jnp.where(lane == idx, arr, 0.0), axis=1, keepdims=True)

    def norm_blocks(k4, _):
        for u in range(4):
            k = k4 * 4 + u
            rows = pl.ds(pl.multiple_of(k * 16, 16), 16)
            normed = (noisy[rows, :] - pick(mi[0], k)) * pick(mi[1], k)
            scl[rows, :] = (normed * gain_ref[...]).astype(BF16)
        return 0

    lax.fori_loop(0, 8, norm_blocks, 0)
    ld_up.wait()
    ld_dn.wait()

    def pre_cols(n):
        res = dot_nn(scl[...], up_v[:, n * 256 : (n + 1) * 256])
        pre[0, :, n * 256 : (n + 1) * 256] = res[0:256]
        pre[1, :, n * 256 : (n + 1) * 256] = res[256:512]
        ugp[:, n * 256 : (n + 1) * 256] = res[512:528]

    pre_cols(0)
    pre_cols(1)
    pre_cols(2)
    cp_pre = rcopy(pre.at[1 - c], pre_in, k_send.at[1], k_recv.at[1], other)
    cp_pre.start()
    cp_ug = rcopy(ugp, ug_in, k_send.at[2], k_recv.at[2], other)
    cp_ug.start()

    def back_chunk(j, ab):
        dim = cg[j, ab].reshape(256, W)
        res = dot_nt(dim, dn_v[:, j * W : (j + 1) * W])
        if j == 0:
            bk[ab] = res
        else:
            bk[ab] = bk[ab] + res

    for j in range(NCH - 1):
        cot_g[j].wait(2)
        for ab in range(2):
            back_chunk(j, ab)
        if j == 0:
            cp_pre.wait_recv()
            cp_ug.wait_recv()
        if j == 1:

            def slope_block(k, _):
                rows = pl.ds(pl.multiple_of(k * 16, 16), 16)
                p = pre[c, rows, :] + pre_in[rows, :]
                pre_in[rows, :] = p
                slope[rows, :] = gelu_slope(p)
                return 0

            lax.fori_loop(0, 16, slope_block, 0)
        if j == 2:
            def wt_block(b, _):
                rr = jnp.where(c == 0, b, swap(b))
                inv = pick(mi[1], c * 16 + b)
                wt[pl.ds(pl.multiple_of(b * 16, 16), 16), :] = jnp.where(
                    lane == rr * 8 + c * 4 + a16, inv, 0.0
                )
                return 0

            lax.fori_loop(0, 16, wt_block, 0)
            full = wt[...].T
            hi = full.astype(BF16)
            mid = (full - hi.astype(F32)).astype(BF16)
            lo = (full - hi.astype(F32) - mid.astype(F32)).astype(BF16)
            wm[0:128] = hi
            wm[128:256] = mid
            wm[256:384] = lo
    cot_g[NCH - 1].wait(2)
    last = NCH - 1
    for flip in (1, 0):
        ab = (c + flip) % 2
        dim = cg[last, ab].reshape(256, W)
        bk[ab] = bk[ab] + dot_nt(dim, dn_v[:, last * W :])
        if flip == 1:
            cp_bk = rcopy(bk.at[1 - c], bk_in, k_send.at[3], k_recv.at[3], other)
            cp_bk.start()
    ug = (ugp[0:1] + ugp[1:2] + ugp[2:3]) + (ug_in[0:1] + ug_in[1:2] + ug_in[2:3])
    cp_bk.wait_recv()

    def hidden_block(b, carry):
        gs, gd = carry
        rows = pl.ds(pl.multiple_of(b * 16, 16), 16)
        hg = ((bk[c, rows, :] + bk_in[rows, :]) * slope[rows, :]).astype(BF16)
        scl[rows, 0:768] = hg
        hf = hg.astype(F32)
        s1 = jnp.sum(hf * ug, axis=1, keepdims=True)
        s2 = jnp.sum(hf * pre_in[rows, :], axis=1, keepdims=True)
        hit = lane == c * 16 + b
        return jnp.where(hit, s1, gs), jnp.where(hit, s2, gd)

    def hidden_blocks(k, carry):
        for u in range(4):
            carry = hidden_block(k * 4 + u, carry)
        return carry

    zero = jnp.zeros((16, 128), F32)
    gst[0], gst[1] = lax.fori_loop(0, 4, hidden_blocks, (zero, zero))
    cp_gst = rcopy(gst, gst_in, k_send.at[4], k_recv.at[4], other)
    cp_gst.start()
    wsum = dot_nn(wm[...], scl[0:256, 0:768])
    wsum = wsum[0:128] + wsum[128:256] + wsum[256:384]
    w_hi = wsum.astype(BF16)
    wx[0:128] = w_hi
    wx[128:256] = (wsum - w_hi.astype(F32)).astype(BF16)
    cp_wx = rcopy(wx, wx_in, k_send.at[5], k_recv.at[5], other)
    cp_wx.start()

    cp_gst.wait_recv()
    gx[...] = gst[...] + gst_in[...]

    @functools.cache
    def g_copy(axis, step):
        src, dst = ((gx, gx_in), (gy, gy_in))[axis]
        k = axis * 3 + step - 1
        return rcopy(src, dst.at[step - 1], g_send.at[k], g_recv.at[k], row_peer(0, axis + 1, step))

    for step in (1, 2, 3):
        g_copy(0, step).start()

    cp_wx.wait_recv()
    wall[...] = (wx[...].astype(F32) + wx_in[...].astype(F32)).astype(BF16)

    far = sorted(range(1, 16), key=lambda k: min(k // 4, 4 - k // 4) + min(k % 4, 4 - k % 4))

    @functools.cache
    def r_copy(ab, k):
        peer = wrap(y + k // 4, 4) * 4 + wrap(x + k % 4, 4)
        return rcopy(rs.at[ab, peer], rr.at[ab, k], r_send.at[ab, k], r_recv.at[ab, k], {"row": peer})

    for ab in range(2):
        for half in range(2):
            q = ab * 2 + half
            o = dot_nt(wall[...], up_v[q * 768 : (q + 1) * 768, :])
            o_s[ab, half] = o[0:128] + o[128:256]

        def pack(k, _, ab=ab):
            rows = pl.ds(pl.multiple_of(k * 8, 8), 8)
            both = jnp.concatenate([o_s[ab, 0, rows, :], o_s[ab, 1, rows, :]], axis=0)
            rs[ab, k] = both.astype(BF16)
            return 0

        lax.fori_loop(0, 16, pack, 0)
        for k in far:
            r_copy(ab, k).start()
        if ab == 0:
            for step in (1, 2, 3):
                g_copy(0, step).wait_recv()
            gy[...] = gx[...] + gx_in[0] + gx_in[1] + gx_in[2]
            for step in (1, 2, 3):
                g_copy(1, step).start()

    for step in (1, 2, 3):
        g_copy(1, step).wait_recv()
    gtot = (gy[...] + gy_in[0] + gy_in[1] + gy_in[2]) * (1.0 / D)
    own_b = (y * 4 + x, x * 4 + y)
    for tok in range(2):
        k = tok * 16 + own_b[tok]
        rows = pl.ds(pl.multiple_of(tok * 256 + own_b[tok] * 16, 16), 16)
        inv = pick(mi[1], k)
        normed = (noisy[rows, :] - pick(mi[0], k)) * inv
        v = inv * (pick(gtot[0], k) + normed * pick(gtot[1], k))
        pk32[tok * 16 : tok * 16 + 16, :] = v
    rest = pk32[...]
    t1 = rest.astype(BF16)
    t2 = (rest - t1.astype(F32)).astype(BF16)
    t3 = (rest - t1.astype(F32) - t2.astype(F32)).astype(BF16)
    pick8 = oh8[:, 0:32]
    rest8 = (dot_nn(pick8, t1) + dot_nn(pick8, t2) + dot_nn(pick8, t3))[0:8]

    own_rows = pl.ds(pl.multiple_of(r * 8, 8), 8)
    for ab in range(2):
        tot = [o_s[ab, half, own_rows, :] for half in range(2)]
        for k in far:
            r_copy(ab, k).wait_recv()
            got = rr[ab, k].astype(F32)
            tot = [tot[half] + got[half * 8 : half * 8 + 8] for half in range(2)]
        for half in range(2):
            lo = ab * 1536 + half * 768
            fin = (tot[half] * gain_ref[:, lo : lo + 768] - rest8[:, lo : lo + 768]) / cnt8
            la_own[0, :, lo : lo + 768] = fin[0:4].astype(BF16)
            la_own[1, :, lo : lo + 768] = fin[4:8].astype(BF16)

    ld_la = pltpu.make_async_copy(la_own, outb_hbm.at[pl.ds(2 * z, 2)], load_sem.at[5])
    ld_la.start()
    la = {s: rcopy(la_own, outb_hbm.at[pl.ds(2 * z, 2)], l_send.at[s], l_recv.at[s], z_peer(s)) for s in z_order}
    for s in (4, 3, 5, 2, 6, 1, 7):
        la[s].start()
    for s in z_order:
        ea[s].wait_recv()
    ld_ea.wait()
    for s in z_order:
        la[s].wait_recv()
    for cp in live:
        cp.wait_send()
    ld_la.wait()


def body(images, gain, up_weight, down_weight, cotangent, seeds, assign):
    W = 3072 // NCH
    vm, dma = pltpu.VMEM, pltpu.SemaphoreType.DMA
    anyspace = pl.BlockSpec(memory_space=pl.ANY)
    early, late = pl.pallas_call(
        kernel,
        out_shape=[jax.ShapeDtypeStruct((16, 4, 3072), F32), jax.ShapeDtypeStruct((16, 4, 3072), BF16)],
        in_specs=[
            anyspace,
            pl.BlockSpec(memory_space=pltpu.VMEM),
            anyspace,
            anyspace,
            anyspace,
            pl.BlockSpec(memory_space=pltpu.SMEM),
            pl.BlockSpec(memory_space=pltpu.SMEM),
        ],
        out_specs=[anyspace, anyspace],
        scratch_shapes=[
            vm((3072, 768), BF16),
            vm((768, 3072), BF16),
            vm((2, 4, 3072), BF16),
            vm((16, 1536), F32),
            vm((2, 2, 4, 4, 16, 384), BF16),
            vm((8, 2, 2, 3072), BF16),
            vm((8, 8, 128), I32),
            vm((32, 3072), F32),
            vm((NCH, 2, 4, 4, 16, W), BF16),
            vm((2, 2, 512, 256), BF16),
            vm((16, 3072), I32),
            vm((512, 3072), F32),
            vm((528, 3072), BF16),
            vm((2, 256, 768), F32),
            vm((256, 768), F32),
            vm((16, 768), F32),
            vm((16, 768), F32),
            vm((256, 768), F32),
            vm((2, 256, 768), F32),
            vm((256, 768), F32),
            vm((2, 16, 128), F32),
            vm((2, 16, 128), F32),
            vm((2, 16, 128), F32),
            vm((2, 16, 128), F32),
            vm((2, 16, 128), F32),
            vm((256, 128), F32),
            vm((384, 256), BF16),
            vm((256, 768), BF16),
            vm((256, 768), BF16),
            vm((256, 768), BF16),
            vm((2, 2, 128, 768), F32),
            vm((2, 16, 16, 768), BF16),
            vm((2, 16, 16, 768), BF16),
            vm((2, 16, 128), F32),
            vm((3, 2, 16, 128), F32),
            vm((2, 16, 128), F32),
            vm((3, 2, 16, 128), F32),
            vm((16, 128), BF16),
            vm((2, 4, 3072), F32),
            vm((2, 4, 3072), BF16),
            dma((6,)),
            dma((8,)), dma((8,)),
            dma((8,)), dma((8,)),
            dma((2, 12)), dma((2, 12)),
            dma((NCH, 12)), dma((NCH, 12)),
            dma((6,)), dma((6,)),
            dma((2, 16)), dma((2, 16)),
            dma((6,)), dma((6,)),
            dma((8,)), dma((8,)),
            dma((8,)), dma((8,)),
        ],
        compiler_params=pltpu.CompilerParams(
            collective_id=0, has_side_effects=True, vmem_limit_bytes=56 * 1024 * 1024
        ),
        cost_estimate=pl.CostEstimate(flops=8 * 10**9, bytes_accessed=12 * 10**6, transcendentals=200000),
    )(images, gain.reshape(1, -1), up_weight, down_weight, cotangent, seeds, assign.reshape(-1))
    return early + late.astype(F32)


def solution(mesh):
    placed = (
        P("row", None, "col"),
        P("col"),
        P("col", "row"),
        P("row", "col"),
        P("row", "noise", "col"),
        P("noise"),
        P(),
    )
    return jax.shard_map(
        body, mesh=mesh, in_specs=placed, out_specs=P("row", None, "col"), check_vma=False
    )
```

```python
import math

import jax
import jax.numpy as jnp
from jax import lax
from jax.experimental import pallas as pl
from jax.experimental.pallas import tpu as pltpu
from jax.sharding import PartitionSpec as P

D = 6144
NJ = 2
NCH = 2 * NJ
WH = 3072 // (2 * NJ)
noise_scale = 0.6
gelu_coef = 0.044715
root_term = math.sqrt(2.0 / math.pi)
MESH = pl.DeviceIdType.MESH
F32 = jnp.float32
BF16 = jnp.bfloat16
I32 = jnp.int32


def gelu_slope(preact):
    inner = root_term * (preact + gelu_coef * preact * preact * preact)
    tanh_val = jnp.tanh(inner)
    return 0.5 * (1.0 + tanh_val) + 0.5 * preact * (1.0 - tanh_val * tanh_val) * root_term * (
        1.0 + 3.0 * gelu_coef * preact * preact
    )


def dot_nt(a, b):
    return lax.dot_general(a, b, (((1,), (1,)), ((), ())), preferred_element_type=F32)


def dot_nn(a, b):
    return lax.dot_general(a, b, (((1,), (0,)), ((), ())), preferred_element_type=F32)


class Copy:
    def __init__(self, live, src, dst, ssem, rsem, dev):
        self.live, self.got = live, False
        self.make = lambda: pltpu.make_async_remote_copy(
            src_ref=src, dst_ref=dst, send_sem=ssem, recv_sem=rsem, device_id=dev, device_id_type=MESH
        )

    def start(self):
        self.made = self.make()
        self.made.start()
        self.live.append(self)

    def wait_recv(self):
        self.made.wait_recv()
        self.got = True

    def wait_send(self):
        self.made.wait_send()


def wrap(i, n):
    return lax.rem(i + n, n)


def kernel(
    img_hbm, gain_ref, up_hbm, dn_hbm, cot_hbm, seeds_ref, assign_ref, outa_hbm, outb_hbm,
    up_v, dn_v, img_own, pk16, imgg, rc, seedg, pk32, cg, onehot, base, noisy, scl,
    pre, pre_in, ugp, ug_in, slope, bk, bk_in, stat, stat_in, mi, gst, gst_in, wt, wm, hgb, wall,
    o_s, rs, rr, gx, gx_in, gy, gy_in, ohs, ea_own, la_own,
    load_sem, z_send, z_recv, s_send, s_recv, i_send, i_recv, c_send, c_recv, k_send, k_recv,
    r_send, r_recv, g_send, g_recv, e_send, e_recv, l_send, l_recv,
):
    z = lax.axis_index("noise")
    r = lax.axis_index("row")
    c = lax.axis_index("col")
    y, x = r // 4, lax.rem(r, 4)
    p1 = (x, y)
    p2 = (y, x)

    def row_peer(ab, phase, step):
        along_x = (ab == 0) == (phase == 1)
        if along_x:
            return {"row": y * 4 + wrap(x + step, 4)}
        return {"row": wrap(y + step, 4) * 4 + x}

    def z_peer(step):
        return {"noise": wrap(z + step, 8)}

    other = {"col": 1 - c}

    live = []

    def rcopy(src, dst, ssem, rsem, dev):
        return Copy(live, src, dst, ssem, rsem, dev)

    ld_img = pltpu.make_async_copy(img_hbm.at[pl.ds(2 * z, 2)], img_own, load_sem.at[0])
    ld_img.start()
    ld_cot = pltpu.make_async_copy(cot_hbm.at[pl.ds(2 * z, 2)], rc.at[z], load_sem.at[1])
    ld_cot.start()
    ld_up = pltpu.make_async_copy(up_hbm, up_v, load_sem.at[2])
    ld_up.start()
    ld_dn = pltpu.make_async_copy(dn_hbm, dn_v, load_sem.at[3])
    ld_dn.start()

    barrier = pltpu.get_barrier_semaphore()
    for dev in (
        [z_peer(s) for s in range(1, 8)]
        + [{"row": wrap(y + k // 4, 4) * 4 + wrap(x + k % 4, 4)} for k in range(1, 16)]
        + [other]
    ):
        pl.semaphore_signal(barrier, inc=1, device_id=dev, device_id_type=MESH)

    seedg[z] = jnp.where(
        lax.broadcasted_iota(I32, (8, 128), 0) == 0, seeds_ref[0], seeds_ref[1]
    )
    ld_img.wait()
    for tok in range(2):
        v = img_own[tok].astype(F32)
        for q in range(4):
            ab, half = q // 2, q % 2
            pk16[half * 8 + tok * 4 : half * 8 + tok * 4 + 4, ab * 768 : (ab + 1) * 768] = v[
                :, q * 768 : (q + 1) * 768
            ]
    for ch in range(2):
        for ab in range(2):
            lo = ab * 768 + ch * 384
            imgg[ch, ab, p2[ab], p1[ab]] = pk16[:, lo : lo + 384].astype(BF16)
    pl.semaphore_wait(barrier, 23)

    z_order = (1, 7, 2, 6, 3, 5, 4)
    z_cot, z_seed = {}, {}
    for s in z_order:
        peer = wrap(z + s, 8)
        z_cot[s] = rcopy(cot_hbm.at[pl.ds(2 * peer, 2)], rc.at[z], z_send.at[s], z_recv.at[s], z_peer(s))
        z_seed[s] = rcopy(seedg.at[z], seedg.at[z], s_send.at[s], s_recv.at[s], z_peer(s))
        z_cot[s].start()
        z_seed[s].start()

    class Gather:
        def __init__(self, buf, ssem, rsem):
            self.copies = {}
            for ab in range(2):
                for phase in (1, 2):
                    own = buf.at[ab, p2[ab], p1[ab]] if phase == 1 else buf.at[ab, p2[ab]]
                    for step in (1, 3, 2):
                        k = (ab * 2 + phase - 1) * 3 + step - 1
                        self.copies[ab, phase, step] = rcopy(
                            own, own, ssem.at[k], rsem.at[k], row_peer(ab, phase, step)
                        )

        def start(self, phase):
            for step in (1, 3, 2):
                for ab in range(2):
                    self.copies[ab, phase, step].start()

        def wait(self, phase):
            for step in (1, 3, 2):
                for ab in range(2):
                    self.copies[ab, phase, step].wait_recv()

    img_g = [Gather(imgg.at[ch], i_send.at[ch], i_recv.at[ch]) for ch in range(2)]
    cot_g = [Gather(cg.at[j], c_send.at[j], c_recv.at[j]) for j in range(NCH)]

    for g in img_g:
        g.start(1)

    sub16 = lax.broadcasted_iota(I32, (16, 128), 0)
    lane = lax.broadcasted_iota(I32, (16, 128), 1)
    a16 = jnp.zeros((16, 128), I32)
    for s in range(16):
        a16 = jnp.where(sub16 == s, assign_ref[s], a16)
    cnt = [jnp.float32(0.0)] * 4
    for s in range(16):
        for i in range(4):
            cnt[i] = cnt[i] + jnp.where(assign_ref[s] == i, 1.0, 0.0)
    counts = jnp.ones((16, 128), F32)
    for i in range(4):
        counts = jnp.where(sub16 == i, cnt[i], counts)
    cnt4 = counts[0:4, 0:1]
    sel = jnp.zeros((16, 128), F32)
    for s in range(16):
        sel = jnp.where((lane == s) & (sub16 == assign_ref[s]), 1.0, sel)
    ohs[...] = sel.astype(BF16)

    def swap(b):
        return lax.rem(b, 4) * 4 + b // 4

    a16w = jnp.concatenate([a16, a16], axis=1)
    col16 = lax.broadcasted_iota(I32, (16, 256), 1)
    for tok in range(2):
        for ab in range(2):
            for half in range(2):

                def fill(b, _, tok=tok, ab=ab, half=half):
                    blk = b if ab == 0 else swap(b)
                    target = a16w + (blk * 16 + half * 8 + tok * 4)
                    onehot[ab, half, pl.ds(pl.multiple_of(tok * 256 + b * 16, 16), 16), :] = jnp.where(
                        col16 == target, 1.0, 0.0
                    ).astype(BF16)
                    return 0

                lax.fori_loop(0, 16, fill, 0)

    for g in img_g:
        g.wait(1)
        g.start(2)

    for s in z_order:
        z_cot[s].wait_recv()
        z_seed[s].wait_recv()
    ld_cot.wait()
    for k in range(8):
        for tok in range(2):
            pk32[tok * 16 + 2 * k : tok * 16 + 2 * k + 2, :] = rc[k, tok].astype(F32)
    for j in range(NCH):
        for ab in range(2):
            tok, lo = j // NJ, (j % NJ) * 2 * WH + ab * WH
            cg[j, ab, p2[ab], p1[ab]] = pk32[tok * 16 : tok * 16 + 16, lo : lo + WH].astype(BF16)
        cot_g[j].start(1)
    for tok in range(2):
        early = dot_nn(ohs[:, 0:16], pk32[tok * 16 : tok * 16 + 16, :].astype(BF16))
        ea_own[tok] = early[0:4] / cnt4
    ld_ea = pltpu.make_async_copy(ea_own, outa_hbm.at[pl.ds(2 * z, 2)], load_sem.at[4])
    ld_ea.start()
    ea = {s: rcopy(ea_own, outa_hbm.at[pl.ds(2 * z, 2)], e_send.at[s], e_recv.at[s], z_peer(s)) for s in z_order}
    for s in z_order:
        ea[s].start()

    for k in range(8):
        for e in range(2):
            s = 2 * k + e
            pos = lax.broadcasted_iota(I32, (1, 3072), 1)
            row = seedg[k, e : e + 1, 0:1] * 1013904223
            base[s : s + 1, :] = (pos + c * 3072) * 1664525 + row

    g0 = gain_ref[...]
    g_hi = g0.astype(BF16)
    g_mid = (g0 - g_hi.astype(F32)).astype(BF16)
    g_lo = (g0 - g_hi.astype(F32) - g_mid.astype(F32)).astype(BF16)
    sub_g = lax.broadcasted_iota(I32, (16, 3072), 0)
    scl[512:528, :] = jnp.where(
        sub_g == 0,
        g_hi.astype(F32),
        jnp.where(sub_g == 1, g_mid.astype(F32), jnp.where(sub_g == 2, g_lo.astype(F32), 0.0)),
    ).astype(BF16)

    for ch in range(2):
        img_g[ch].wait(2)
        for ab in range(2):
            for half in range(2):
                lo = ab * 1536 + half * 768 + ch * 384
                noisy[:, lo : lo + 384] = dot_nn(onehot[ab, half], imgg[ch, ab].reshape(256, 384))

    def pump(k):
        cot_g[k].wait(1)
        cot_g[k].start(2)

    pump(0)

    def token_of(tok, b):
        return b * 16 + z * 2 + tok

    def noise_block(tok, b, carry):
        tot, m2 = carry
        rows = pl.ds(pl.multiple_of(tok * 256 + b * 16, 16), 16)
        mixed = base[...] + token_of(tok, b) * D * 1664525
        mixed = mixed ^ (mixed >> 13)
        mixed = mixed * 1274126177
        mixed = mixed ^ (mixed >> 16)
        field = (mixed & 65535).astype(F32) - 32767.5
        v = noisy[rows, :] + field * (noise_scale / 18918.0)
        noisy[rows, :] = v
        s1 = jnp.sum(v, axis=1, keepdims=True)
        dev = v - s1 * (1.0 / 3072.0)
        s2 = jnp.sum(dev * dev, axis=1, keepdims=True)
        hit = lane == tok * 16 + b
        return jnp.where(hit, s1, tot), jnp.where(hit, s2, m2)

    carry = (jnp.zeros((16, 128), F32), jnp.zeros((16, 128), F32))
    def noise_blocks(tok, first, carry):
        def four(k, cr):
            for u in range(4):
                cr = noise_block(tok, first + k * 4 + u, cr)
            return cr

        return lax.fori_loop(0, 2, four, carry)

    carry = noise_blocks(0, 0, carry)
    pump(1)
    carry = noise_blocks(0, 8, carry)
    pump(2)
    carry = noise_blocks(1, 0, carry)
    pump(3)
    carry = noise_blocks(1, 8, carry)
    stat[0], stat[1] = carry
    cp_stat = rcopy(stat, stat_in, k_send.at[1, 1], k_recv.at[1, 1], other)
    cp_stat.start()
    cp_stat.wait_recv()
    mean_a, mean_b = stat[0] * (1.0 / 3072.0), stat_in[0] * (1.0 / 3072.0)
    gap = mean_a - mean_b
    var = (stat[1] + stat_in[1] + gap * gap * 1536.0) * (1.0 / D)
    mi[0] = (mean_a + mean_b) * 0.5
    mi[1] = lax.rsqrt(var + 1e-06)

    def pick(arr, idx):
        return jnp.sum(jnp.where(lane == idx, arr, 0.0), axis=1, keepdims=True)

    def norm_blocks(k4, _):
        for u in range(4):
            k = k4 * 4 + u
            rows = pl.ds(pl.multiple_of(k * 16, 16), 16)
            normed = (noisy[rows, :] - pick(mi[0], k)) * pick(mi[1], k)
            scl[rows, :] = (normed * gain_ref[...]).astype(BF16)
        return 0

    lax.fori_loop(0, 8, norm_blocks, 0)
    ld_up.wait()
    ld_dn.wait()

    def pre_cols(n):
        res = dot_nn(scl[...], up_v[:, n * 256 : (n + 1) * 256])
        for tok in range(2):
            for h in range(2):
                lo = tok * 256 + h * 128
                pre[tok, h, :, n * 256 : (n + 1) * 256] = res[lo : lo + 128]
        ugp[:, n * 256 : (n + 1) * 256] = res[512:528]

    pre_cols(0)
    pre_cols(1)
    pre_cols(2)
    cp_pre = [
        rcopy(pre.at[tok, 1 - c], pre_in.at[tok], k_send.at[0, tok], k_recv.at[0, tok], other) for tok in range(2)
    ]
    for cp in cp_pre:
        cp.start()
    cp_ug = rcopy(ugp, ug_in, k_send.at[1, 0], k_recv.at[1, 0], other)
    cp_ug.start()

    def back_chunk(k):
        tok = k // NJ
        cot_g[k].wait(2)
        for ab in range(2):
            lo = (k % NJ) * 2 * WH + ab * WH
            res = dot_nt(cg[k, ab].reshape(256, WH), dn_v[:, lo : lo + WH])
            for b in range(16):
                at = b if ab == 0 else (b % 4) * 4 + b // 4
                part = res[at * 16 : at * 16 + 16]
                h, lb = b // 8, (b % 8) * 16
                if k % NJ == 0 and ab == 0:
                    bk[tok, h, lb : lb + 16] = part
                else:
                    bk[tok, h, lb : lb + 16] = bk[tok, h, lb : lb + 16] + part

    cp_bk = [rcopy(bk.at[tok, 1 - c], bk_in.at[tok], k_send.at[2, tok], k_recv.at[2, tok], other) for tok in range(2)]
    cp_gst = [rcopy(gst.at[tok], gst_in.at[tok], k_send.at[3, tok], k_recv.at[3, tok], other) for tok in range(2)]
    cp_w = [
        rcopy(wall.at[tok, c], wall.at[tok, c], k_send.at[4, tok], k_recv.at[4, tok], other) for tok in range(2)
    ]

    def g_copy(tok, axis, step):
        src, dst = ((gx, gx_in), (gy, gy_in))[axis]
        k = axis * 3 + step - 1
        return rcopy(
            src.at[tok], dst.at[tok, step - 1], g_send.at[tok, k], g_recv.at[tok, k], row_peer(0, axis + 1, step)
        )

    g_all = {
        (tok, axis, step): g_copy(tok, axis, step) for tok in range(2) for axis in range(2) for step in (1, 2, 3)
    }
    far = sorted(range(1, 16), key=lambda k: min(k // 4, 4 - k // 4) + min(k % 4, 4 - k % 4))

    def r_copy(tok, k):
        peer = wrap(y + k // 4, 4) * 4 + wrap(x + k % 4, 4)
        return rcopy(rs.at[tok, peer], rr.at[tok, k], r_send.at[tok, k], r_recv.at[tok, k], {"row": peer})

    r_all = {(tok, k): r_copy(tok, k) for tok in range(2) for k in far}
    la = {
        (tok, s): rcopy(
            la_own.at[tok], outb_hbm.at[2 * z + tok], l_send.at[tok, s], l_recv.at[tok, s], z_peer(s)
        )
        for tok in range(2)
        for s in z_order
    }

    for tok in range(2):
        cp_pre[tok].wait_recv()
    cp_ug.wait_recv()
    for tok in range(2):

        def slope_block(k, _, tok=tok):
            for u in range(2):
                rows = pl.ds(pl.multiple_of(k * 32 + u * 16, 16), 16)
                p = pre[tok, c, rows, :] + pre_in[tok, rows, :]
                pre_in[tok, rows, :] = p
                slope[tok, rows, :] = gelu_slope(p)
            return 0

        lax.fori_loop(0, 4, slope_block, 0)
    ug = (ugp[0:1] + ugp[1:2] + ugp[2:3]) + (ug_in[0:1] + ug_in[1:2] + ug_in[2:3])
    for tok in range(2):
        for b in range(8):
            inv = pick(mi[1], tok * 16 + c * 8 + b)
            wt[b * 16 : b * 16 + 16, :] = jnp.where(lane == b * 4 + a16, inv, 0.0)
        full = wt[...].T[0:32]
        hi = full.astype(BF16)
        mid = (full - hi.astype(F32)).astype(BF16)
        lo = (full - hi.astype(F32) - mid.astype(F32)).astype(BF16)
        wm[tok, 0:32] = hi
        wm[tok, 32:64] = mid
        wm[tok, 64:96] = lo

    def hidden(tok):
        cp_bk[tok].wait_recv()

        def hidden_blocks(k, carry):
            gs, gd = carry
            for u in range(4):
                b = k * 4 + u
                rows = pl.ds(pl.multiple_of(b * 16, 16), 16)
                hg = ((bk[tok, c, rows, :] + bk_in[tok, rows, :]) * slope[tok, rows, :]).astype(BF16)
                hgb[tok, rows, :] = hg
                hf = hg.astype(F32)
                s1 = jnp.sum(hf * ug, axis=1, keepdims=True)
                s2 = jnp.sum(hf * pre_in[tok, rows, :], axis=1, keepdims=True)
                hit = lane == c * 8 + b
                gs, gd = jnp.where(hit, s1, gs), jnp.where(hit, s2, gd)
            return gs, gd

        zero = jnp.zeros((16, 128), F32)
        gst[tok, 0], gst[tok, 1] = lax.fori_loop(0, 2, hidden_blocks, (zero, zero))
        wsum = dot_nn(wm[tok], hgb[tok])
        wsum = wsum[0:32] + wsum[32:64] + wsum[64:96]
        w_hi = wsum.astype(BF16)
        wall[tok, c, 0] = w_hi
        wall[tok, c, 1] = (wsum - w_hi.astype(F32)).astype(BF16)
        cp_w[tok].start()
        cp_gst[tok].start()

    def spread(tok):
        cp_w[tok].wait_recv()
        cp_gst[tok].wait_recv()
        gx[tok] = gst[tok] + gst_in[tok]
        for step in (1, 2, 3):
            g_all[tok, 0, step].start()
        for q in range(4):
            o = dot_nt(wall[tok].reshape(128, 768), up_v[q * 768 : (q + 1) * 768, :])
            o_s[tok, q, 0:32] = o[0:32] + o[32:64]
            o_s[tok, q, 32:64] = o[64:96] + o[96:128]

        def pack(k, _):
            rows = pl.ds(pl.multiple_of(k * 8, 8), 8)
            v = [o_s[tok, q, rows, :] for q in range(4)]
            for u in range(2):
                rs[tok, k * 2 + u] = jnp.concatenate([w[u * 4 : u * 4 + 4] for w in v], axis=0).astype(BF16)
            return 0

        lax.fori_loop(0, 8, pack, 0)
        for k in far:
            r_all[tok, k].start()

    def sums_y(tok):
        for step in (1, 2, 3):
            g_all[tok, 0, step].wait_recv()
        gy[tok] = gx[tok] + gx_in[tok, 0] + gx_in[tok, 1] + gx_in[tok, 2]
        for step in (1, 2, 3):
            g_all[tok, 1, step].start()

    def finish(tok):
        for step in (1, 2, 3):
            g_all[tok, 1, step].wait_recv()
        gtot = (gy[tok] + gy_in[tok, 0] + gy_in[tok, 1] + gy_in[tok, 2]) * (1.0 / D)
        rows = pl.ds(pl.multiple_of(tok * 256 + r * 16, 16), 16)
        inv = pick(mi[1], tok * 16 + r)
        normed = (noisy[rows, :] - pick(mi[0], tok * 16 + r)) * inv
        v = inv * (pick(gtot[0], r) + normed * pick(gtot[1], r))
        t1 = v.astype(BF16)
        t2 = (v - t1.astype(F32)).astype(BF16)
        t3 = (v - t1.astype(F32) - t2.astype(F32)).astype(BF16)
        one = ohs[:, 0:16]
        rest4 = (dot_nn(one, t1) + dot_nn(one, t2) + dot_nn(one, t3))[0:4]
        tot = rs[tok, r].astype(F32)
        for k in far:
            r_all[tok, k].wait_recv()
            tot = tot + rr[tok, k].astype(F32)
        for q in range(4):
            lo = q * 768
            fin = (tot[q * 4 : q * 4 + 4] * gain_ref[:, lo : lo + 768] - rest4[:, lo : lo + 768]) / cnt4
            la_own[tok, :, lo : lo + 768] = fin.astype(BF16)
        for s in (4, 3, 5, 2, 6, 1, 7):
            la[tok, s].start()

    for k in range(NJ):
        back_chunk(k)
    cp_bk[0].start()
    hidden(0)
    spread(0)
    back_chunk(NJ)
    sums_y(0)
    for k in range(NJ + 1, NCH):
        back_chunk(k)
    cp_bk[1].start()
    hidden(1)
    finish(0)
    spread(1)
    sums_y(1)
    finish(1)
    ld_la = pltpu.make_async_copy(la_own, outb_hbm.at[pl.ds(2 * z, 2)], load_sem.at[5])
    ld_la.start()
    for s in z_order:
        ea[s].wait_recv()
    ld_ea.wait()
    for tok in range(2):
        for s in z_order:
            la[tok, s].wait_recv()
    for cp in live:
        cp.wait_send()
    ld_la.wait()


def body(images, gain, up_weight, down_weight, cotangent, seeds, assign):
    vm, dma = pltpu.VMEM, pltpu.SemaphoreType.DMA
    anyspace = pl.BlockSpec(memory_space=pl.ANY)
    early, late = pl.pallas_call(
        kernel,
        out_shape=[jax.ShapeDtypeStruct((16, 4, 3072), F32), jax.ShapeDtypeStruct((16, 4, 3072), BF16)],
        in_specs=[
            anyspace,
            pl.BlockSpec(memory_space=pltpu.VMEM),
            anyspace,
            anyspace,
            anyspace,
            pl.BlockSpec(memory_space=pltpu.SMEM),
            pl.BlockSpec(memory_space=pltpu.SMEM),
        ],
        out_specs=[anyspace, anyspace],
        scratch_shapes=[
            vm((3072, 768), BF16),
            vm((768, 3072), BF16),
            vm((2, 4, 3072), BF16),
            vm((16, 1536), F32),
            vm((2, 2, 4, 4, 16, 384), BF16),
            vm((8, 2, 2, 3072), BF16),
            vm((8, 8, 128), I32),
            vm((32, 3072), F32),
            vm((NCH, 2, 4, 4, 16, WH), BF16),
            vm((2, 2, 512, 256), BF16),
            vm((16, 3072), I32),
            vm((512, 3072), F32),
            vm((528, 3072), BF16),
            vm((2, 2, 128, 768), F32),
            vm((2, 128, 768), F32),
            vm((16, 768), F32),
            vm((16, 768), F32),
            vm((2, 128, 768), F32),
            vm((2, 2, 128, 768), F32),
            vm((2, 128, 768), F32),
            vm((2, 16, 128), F32),
            vm((2, 16, 128), F32),
            vm((2, 16, 128), F32),
            vm((2, 2, 16, 128), F32),
            vm((2, 2, 16, 128), F32),
            vm((128, 128), F32),
            vm((2, 96, 128), BF16),
            vm((2, 128, 768), BF16),
            vm((2, 2, 2, 32, 768), BF16),
            vm((2, 4, 64, 768), F32),
            vm((2, 16, 16, 768), BF16),
            vm((2, 16, 16, 768), BF16),
            vm((2, 2, 16, 128), F32),
            vm((2, 3, 2, 16, 128), F32),
            vm((2, 2, 16, 128), F32),
            vm((2, 3, 2, 16, 128), F32),
            vm((16, 128), BF16),
            vm((2, 4, 3072), F32),
            vm((2, 4, 3072), BF16),
            dma((6,)),
            dma((8,)), dma((8,)),
            dma((8,)), dma((8,)),
            dma((2, 12)), dma((2, 12)),
            dma((NCH, 12)), dma((NCH, 12)),
            dma((5, 2)), dma((5, 2)),
            dma((2, 16)), dma((2, 16)),
            dma((2, 6)), dma((2, 6)),
            dma((8,)), dma((8,)),
            dma((2, 8)), dma((2, 8)),
        ],
        compiler_params=pltpu.CompilerParams(
            collective_id=0, has_side_effects=True, vmem_limit_bytes=56 * 1024 * 1024
        ),
        cost_estimate=pl.CostEstimate(flops=8 * 10**9, bytes_accessed=12 * 10**6, transcendentals=200000),
    )(images, gain.reshape(1, -1), up_weight, down_weight, cotangent, seeds, assign.reshape(-1))
    return early + late.astype(F32)


def solution(mesh):
    placed = (
        P("row", None, "col"),
        P("col"),
        P("col", "row"),
        P("row", "col"),
        P("row", "noise", "col"),
        P("noise"),
        P(),
    )
    return jax.shard_map(
        body, mesh=mesh, in_specs=placed, out_specs=P("row", None, "col"), check_vma=False
    )
```

```python
import math

import jax
import jax.numpy as jnp
from jax import lax
from jax.experimental import pallas as pl
from jax.experimental.pallas import tpu as pltpu
from jax.sharding import PartitionSpec as P

D = 6144
noise_scale = 0.6
gelu_coef = 0.044715
root_term = math.sqrt(2.0 / math.pi)
MESH = pl.DeviceIdType.MESH
F32 = jnp.float32
BF16 = jnp.bfloat16
I32 = jnp.int32


def gelu_slope(preact):
    inner = root_term * (preact + gelu_coef * preact * preact * preact)
    tanh_val = jnp.tanh(inner)
    return 0.5 * (1.0 + tanh_val) + 0.5 * preact * (1.0 - tanh_val * tanh_val) * root_term * (
        1.0 + 3.0 * gelu_coef * preact * preact
    )


def dot_nt(a, b):
    return lax.dot_general(a, b, (((1,), (1,)), ((), ())), preferred_element_type=F32)


def dot_nn(a, b):
    return lax.dot_general(a, b, (((1,), (0,)), ((), ())), preferred_element_type=F32)


class Copies:
    def __init__(self, live, ssem, rsem, whole, dev):
        self.live, self.ssem, self.rsem = live, ssem, rsem
        self.whole = lambda: pltpu.make_async_remote_copy(
            src_ref=whole, dst_ref=whole, send_sem=ssem, recv_sem=rsem, device_id=dev, device_id_type=MESH
        )

    def send(self, src, dst, dev):
        if self not in self.live:
            self.live.append(self)
        pltpu.make_async_remote_copy(
            src_ref=src, dst_ref=dst, send_sem=self.ssem, recv_sem=self.rsem, device_id=dev, device_id_type=MESH
        ).start()

    def wait_recv(self):
        self.whole().wait_recv()

    def wait_send(self):
        self.whole().wait_send()


class Copy(Copies):
    def __init__(self, live, src, dst, ssem, rsem, dev):
        super().__init__(live, ssem, rsem, dst, dev)
        self.start = lambda: self.send(src, dst, dev)


def wrap(i, n):
    return lax.rem(i + n, n)


def kernel(
    img_hbm, gain_ref, up_hbm, dn_hbm, cot_hbm, seeds_ref, assign_ref, outa_hbm, outb_hbm,
    up_v, dn_v, img_own, pk16, imgg, rc, seedg, pk32, cg, onehot, base, noisy, scl,
    pre, pre_in, ugp, ug_in, slope, bk, bk_in, stat, stat_in, mi, gst, gst_in, wt, wm, hgb, wall,
    o_s, rs, rr, gx, gx_in, gy, gy_in, ohs, ea_own, la_own,
    load_sem, z_send, z_recv, i_send, i_recv, c_send, c_recv, k_send, k_recv,
    r_send, r_recv, g_send, g_recv, e_send, e_recv, l_send, l_recv,
):
    z = lax.axis_index("noise")
    r = lax.axis_index("row")
    c = lax.axis_index("col")
    y, x = r // 4, lax.rem(r, 4)
    p1 = (x, y)
    p2 = (y, x)

    def row_peer(ab, phase, step):
        along_x = (ab == 0) == (phase == 1)
        if along_x:
            return {"row": y * 4 + wrap(x + step, 4)}
        return {"row": wrap(y + step, 4) * 4 + x}

    def z_peer(step):
        return {"noise": wrap(z + step, 8)}

    other = {"col": 1 - c}

    live = []

    def rcopy(src, dst, ssem, rsem, dev):
        return Copy(live, src, dst, ssem, rsem, dev)

    ld_img = pltpu.make_async_copy(img_hbm.at[pl.ds(2 * z, 2)], img_own, load_sem.at[0])
    ld_img.start()
    ld_cot = pltpu.make_async_copy(cot_hbm.at[pl.ds(2 * z, 2)], rc.at[z], load_sem.at[1])
    ld_cot.start()
    ld_up = pltpu.make_async_copy(up_hbm, up_v, load_sem.at[2])
    ld_up.start()
    ld_dn = pltpu.make_async_copy(dn_hbm, dn_v, load_sem.at[3])
    ld_dn.start()

    barrier = pltpu.get_barrier_semaphore()
    for dev in (
        [z_peer(s) for s in range(1, 8)]
        + [{"row": wrap(y + k // 4, 4) * 4 + wrap(x + k % 4, 4)} for k in range(1, 16)]
        + [other]
    ):
        pl.semaphore_signal(barrier, inc=1, device_id=dev, device_id_type=MESH)

    seedg[z] = jnp.where(
        lax.broadcasted_iota(I32, (8, 128), 0) == 0, seeds_ref[0], seeds_ref[1]
    )
    ld_img.wait()
    for tok in range(2):
        v = img_own[tok].astype(F32)
        for q in range(4):
            ab, half = q // 2, q % 2
            pk16[half * 8 + tok * 4 : half * 8 + tok * 4 + 4, ab * 768 : (ab + 1) * 768] = v[
                :, q * 768 : (q + 1) * 768
            ]
    for ab in range(2):
        imgg[ab, p2[ab], p1[ab]] = pk16[:, ab * 768 : ab * 768 + 768].astype(BF16)
    pl.semaphore_wait(barrier, 23)

    z_order = (1, 7, 2, 6, 3, 5, 4)
    z_seed = Copies(live, z_send.at[0], z_recv.at[0], seedg.at[pl.ds(0, 7)], z_peer(1))
    z_cot = Copies(live, z_send.at[1], z_recv.at[1], rc.at[pl.ds(0, 7)], z_peer(1))
    for s in z_order:
        z_seed.send(seedg.at[z], seedg.at[z], z_peer(s))
    for s in z_order:
        z_cot.send(cot_hbm.at[pl.ds(2 * wrap(z + s, 8), 2)], rc.at[z], z_peer(s))

    class Gather:
        def __init__(self, buf, ssem, rsem):
            three = pl.ds(0, 3)
            whole = (buf.at[pl.ds(0, 2), 0, three], buf.at[pl.ds(0, 2), three])
            self.buf = buf
            self.copies = [
                Copies(live, ssem.at[n], rsem.at[n], whole[n], row_peer(0, n + 1, 1)) for n in range(2)
            ]

        def start(self, phase):
            for step in (1, 3, 2):
                for ab in range(2):
                    own = self.buf.at[ab, p2[ab], p1[ab]] if phase == 1 else self.buf.at[ab, p2[ab]]
                    self.copies[phase - 1].send(own, own, row_peer(ab, phase, step))

        def wait(self, phase):
            self.copies[phase - 1].wait_recv()

    img_g = Gather(imgg, i_send, i_recv)
    cot_g = [Gather(cg.at[j], c_send.at[j], c_recv.at[j]) for j in range(2)]

    img_g.start(1)

    sub16 = lax.broadcasted_iota(I32, (16, 128), 0)
    lane = lax.broadcasted_iota(I32, (16, 128), 1)
    a16 = jnp.zeros((16, 128), I32)
    for s in range(16):
        a16 = jnp.where(sub16 == s, assign_ref[s], a16)
    cnt = [jnp.float32(0.0)] * 4
    for s in range(16):
        for i in range(4):
            cnt[i] = cnt[i] + jnp.where(assign_ref[s] == i, 1.0, 0.0)
    counts = jnp.ones((16, 128), F32)
    for i in range(4):
        counts = jnp.where(sub16 == i, cnt[i], counts)
    cnt4 = counts[0:4, 0:1]
    sel = jnp.zeros((16, 128), F32)
    for s in range(16):
        sel = jnp.where((lane == s) & (sub16 == assign_ref[s]), 1.0, sel)
    ohs[...] = sel.astype(BF16)

    def swap(b):
        return lax.rem(b, 4) * 4 + b // 4

    a16w = jnp.concatenate([a16, a16], axis=1)
    col16 = lax.broadcasted_iota(I32, (16, 256), 1)
    for tok in range(2):
        for ab in range(2):
            for half in range(2):

                def fill(b, _, tok=tok, ab=ab, half=half):
                    blk = b if ab == 0 else swap(b)
                    target = a16w + (blk * 16 + half * 8 + tok * 4)
                    onehot[ab, half, pl.ds(pl.multiple_of(tok * 256 + b * 16, 16), 16), :] = jnp.where(
                        col16 == target, 1.0, 0.0
                    ).astype(BF16)
                    return 0

                lax.fori_loop(0, 16, fill, 0)

    img_g.wait(1)
    img_g.start(2)

    g0 = gain_ref[...]
    g_hi = g0.astype(BF16)
    g_mid = (g0 - g_hi.astype(F32)).astype(BF16)
    g_lo = (g0 - g_hi.astype(F32) - g_mid.astype(F32)).astype(BF16)
    sub_g = lax.broadcasted_iota(I32, (16, 3072), 0)
    scl[512:528, :] = jnp.where(
        sub_g == 0,
        g_hi.astype(F32),
        jnp.where(sub_g == 1, g_mid.astype(F32), jnp.where(sub_g == 2, g_lo.astype(F32), 0.0)),
    ).astype(BF16)
    z_seed.wait_recv()
    for k in range(8):
        for e in range(2):
            s = 2 * k + e
            pos = lax.broadcasted_iota(I32, (1, 3072), 1)
            row = seedg[k, e : e + 1, 0:1] * 1013904223
            base[s : s + 1, :] = (pos + c * 3072) * 1664525 + row

    def field_blocks(tok):
        def four(k, _):
            for u in range(4):
                b = k * 4 + u
                mixed = base[...] + (b * 16 + z * 2 + tok) * D * 1664525
                mixed = mixed ^ (mixed >> 13)
                mixed = mixed * 1274126177
                mixed = mixed ^ (mixed >> 16)
                field = (mixed & 65535).astype(F32) - 32767.5
                noisy[pl.ds(pl.multiple_of(tok * 256 + b * 16, 16), 16), :] = field * (noise_scale / 18918.0)
            return 0

        lax.fori_loop(0, 4, four, 0)

    def pack_cot(tok):
        for k in range(8):
            pk32[tok * 16 + 2 * k : tok * 16 + 2 * k + 2, :] = rc[k, tok].astype(F32)
        for ab in range(2):
            cg[tok, ab, p2[ab], p1[ab]] = pk32[tok * 16 : tok * 16 + 16, ab * 1536 : ab * 1536 + 1536].astype(BF16)
        cot_g[tok].start(1)

    def pump(k):
        cot_g[k].wait(1)
        cot_g[k].start(2)

    z_cot.wait_recv()
    ld_cot.wait()
    pack_cot(0)
    pack_cot(1)
    for tok in range(2):
        early = dot_nn(ohs[:, 0:16], pk32[tok * 16 : tok * 16 + 16, :].astype(BF16))
        ea_own[tok] = early[0:4] / cnt4
    ld_ea = pltpu.make_async_copy(ea_own, outa_hbm.at[pl.ds(2 * z, 2)], load_sem.at[4])
    ld_ea.start()
    ea = Copies(live, e_send.at[0], e_recv.at[0], outa_hbm.at[pl.ds(0, 14)], z_peer(1))
    for s in z_order:
        ea.send(ea_own, outa_hbm.at[pl.ds(2 * z, 2)], z_peer(s))
    field_blocks(0)
    field_blocks(1)
    pump(0)
    img_g.wait(2)
    for ab in range(2):
        for half in range(2):
            lo = ab * 1536 + half * 768
            noisy[:, lo : lo + 768] = noisy[:, lo : lo + 768] + dot_nn(
                onehot[ab, half], imgg[ab].reshape(256, 768)
            )
    pump(1)

    def stat_blocks(k, carry):
        tot, m2 = carry
        for u in range(4):
            n = k * 4 + u
            v = noisy[pl.ds(pl.multiple_of(n * 16, 16), 16), :]
            s1 = jnp.sum(v, axis=1, keepdims=True)
            dev = v - s1 * (1.0 / 3072.0)
            s2 = jnp.sum(dev * dev, axis=1, keepdims=True)
            hit = lane == n
            tot, m2 = jnp.where(hit, s1, tot), jnp.where(hit, s2, m2)
        return tot, m2

    carry = lax.fori_loop(0, 8, stat_blocks, (jnp.zeros((16, 128), F32), jnp.zeros((16, 128), F32)))
    stat[0], stat[1] = carry
    cp_stat = rcopy(stat, stat_in, k_send.at[1, 1], k_recv.at[1, 1], other)
    cp_stat.start()
    cp_stat.wait_recv()
    mean_a, mean_b = stat[0] * (1.0 / 3072.0), stat_in[0] * (1.0 / 3072.0)
    gap = mean_a - mean_b
    var = (stat[1] + stat_in[1] + gap * gap * 1536.0) * (1.0 / D)
    mi[0] = (mean_a + mean_b) * 0.5
    mi[1] = lax.rsqrt(var + 1e-06)

    def pick(arr, idx):
        return jnp.sum(jnp.where(lane == idx, arr, 0.0), axis=1, keepdims=True)

    def norm_blocks(k4, _):
        for u in range(4):
            k = k4 * 4 + u
            rows = pl.ds(pl.multiple_of(k * 16, 16), 16)
            normed = (noisy[rows, :] - pick(mi[0], k)) * pick(mi[1], k)
            scl[rows, :] = (normed * gain_ref[...]).astype(BF16)
        return 0

    lax.fori_loop(0, 8, norm_blocks, 0)
    ld_up.wait()
    ld_dn.wait()

    def pre_cols(n):
        res = dot_nn(scl[...], up_v[:, n * 256 : (n + 1) * 256])
        for tok in range(2):
            for h in range(2):
                lo = tok * 256 + h * 128
                pre[tok, h, :, n * 256 : (n + 1) * 256] = res[lo : lo + 128]
        ugp[:, n * 256 : (n + 1) * 256] = res[512:528]

    pre_cols(0)
    pre_cols(1)
    pre_cols(2)
    cp_pre = [
        rcopy(pre.at[tok, 1 - c], pre_in.at[tok], k_send.at[0, tok], k_recv.at[0, tok], other) for tok in range(2)
    ]
    for cp in cp_pre:
        cp.start()
    cp_ug = rcopy(ugp, ug_in, k_send.at[1, 0], k_recv.at[1, 0], other)
    cp_ug.start()

    def back_part(tok):
        cot_g[tok].wait(2)
        for ab in range(2):
            lo = ab * 1536
            res = dot_nt(cg[tok, ab].reshape(256, 1536), dn_v[:, lo : lo + 1536])
            for b in range(16):
                at = b if ab == 0 else (b % 4) * 4 + b // 4
                part = res[at * 16 : at * 16 + 16]
                h, lb = b // 8, (b % 8) * 16
                if ab == 0:
                    bk[tok, h, lb : lb + 16] = part
                else:
                    bk[tok, h, lb : lb + 16] = bk[tok, h, lb : lb + 16] + part

    cp_bk = [rcopy(bk.at[tok, 1 - c], bk_in.at[tok], k_send.at[2, tok], k_recv.at[2, tok], other) for tok in range(2)]
    cp_gst = [rcopy(gst.at[tok], gst_in.at[tok], k_send.at[3, tok], k_recv.at[3, tok], other) for tok in range(2)]
    cp_w = [
        rcopy(wall.at[tok, c], wall.at[tok, c], k_send.at[4, tok], k_recv.at[4, tok], other) for tok in range(2)
    ]

    sums = {
        (tok, axis): Copies(
            live, g_send.at[tok, axis], g_recv.at[tok, axis], (gx_in, gy_in)[axis].at[tok], row_peer(0, axis + 1, 1)
        )
        for tok in range(2)
        for axis in range(2)
    }

    def sums_send(tok, axis):
        src, dst = ((gx, gx_in), (gy, gy_in))[axis]
        for step in (1, 3, 2):
            sums[tok, axis].send(src.at[tok], dst.at[tok, step - 1], row_peer(0, axis + 1, step))

    far = sorted(range(1, 16), key=lambda k: min(k // 4, 4 - k // 4) + min(k % 4, 4 - k % 4))
    parts = [
        Copies(live, r_send.at[tok], r_recv.at[tok], rr.at[tok, pl.ds(1, 15)], row_peer(0, 1, 1)) for tok in range(2)
    ]
    late = [
        Copies(live, l_send.at[tok], l_recv.at[tok], outb_hbm.at[pl.ds(0, 7)], z_peer(1)) for tok in range(2)
    ]

    for tok in range(2):
        cp_pre[tok].wait_recv()
    cp_ug.wait_recv()
    for tok in range(2):

        def slope_block(k, _, tok=tok):
            for u in range(2):
                rows = pl.ds(pl.multiple_of(k * 32 + u * 16, 16), 16)
                p = pre[tok, c, rows, :] + pre_in[tok, rows, :]
                pre_in[tok, rows, :] = p
                slope[tok, rows, :] = gelu_slope(p)
            return 0

        lax.fori_loop(0, 4, slope_block, 0)
    ug = (ugp[0:1] + ugp[1:2] + ugp[2:3]) + (ug_in[0:1] + ug_in[1:2] + ug_in[2:3])
    for tok in range(2):
        for b in range(8):
            inv = pick(mi[1], tok * 16 + c * 8 + b)
            wt[b * 16 : b * 16 + 16, :] = jnp.where(lane == b * 4 + a16, inv, 0.0)
        full = wt[...].T[0:32]
        hi = full.astype(BF16)
        mid = (full - hi.astype(F32)).astype(BF16)
        lo = (full - hi.astype(F32) - mid.astype(F32)).astype(BF16)
        wm[tok, 0:32] = hi
        wm[tok, 32:64] = mid
        wm[tok, 64:96] = lo

    def hidden(tok):
        cp_bk[tok].wait_recv()

        def hidden_blocks(k, carry):
            gs, gd = carry
            for u in range(4):
                b = k * 4 + u
                rows = pl.ds(pl.multiple_of(b * 16, 16), 16)
                hg = ((bk[tok, c, rows, :] + bk_in[tok, rows, :]) * slope[tok, rows, :]).astype(BF16)
                hgb[tok, rows, :] = hg
                hf = hg.astype(F32)
                s1 = jnp.sum(hf * ug, axis=1, keepdims=True)
                s2 = jnp.sum(hf * pre_in[tok, rows, :], axis=1, keepdims=True)
                hit = lane == c * 8 + b
                gs, gd = jnp.where(hit, s1, gs), jnp.where(hit, s2, gd)
            return gs, gd

        zero = jnp.zeros((16, 128), F32)
        gst[tok, 0], gst[tok, 1] = lax.fori_loop(0, 2, hidden_blocks, (zero, zero))
        wsum = dot_nn(wm[tok], hgb[tok])
        wsum = wsum[0:32] + wsum[32:64] + wsum[64:96]
        w_hi = wsum.astype(BF16)
        wall[tok, c, 0] = w_hi
        wall[tok, c, 1] = (wsum - w_hi.astype(F32)).astype(BF16)
        cp_w[tok].start()
        cp_gst[tok].start()

    def spread(tok):
        cp_w[tok].wait_recv()
        cp_gst[tok].wait_recv()
        gx[tok] = gst[tok] + gst_in[tok]
        sums_send(tok, 0)
        for q in range(4):
            o = dot_nt(wall[tok].reshape(128, 768), up_v[q * 768 : (q + 1) * 768, :])
            o_s[tok, q, 0:32] = o[0:32] + o[32:64]
            o_s[tok, q, 32:64] = o[64:96] + o[96:128]

        def pack(k, _):
            rows = pl.ds(pl.multiple_of(k * 8, 8), 8)
            v = [o_s[tok, q, rows, :] for q in range(4)]
            for u in range(2):
                rs[tok, k * 2 + u] = jnp.concatenate([w[u * 4 : u * 4 + 4] for w in v], axis=0).astype(BF16)
            return 0

        lax.fori_loop(0, 8, pack, 0)
        for k in far:
            peer = wrap(y + k // 4, 4) * 4 + wrap(x + k % 4, 4)
            parts[tok].send(rs.at[tok, peer], rr.at[tok, k], {"row": peer})

    def sums_y(tok):
        sums[tok, 0].wait_recv()
        gy[tok] = gx[tok] + gx_in[tok, 0] + gx_in[tok, 1] + gx_in[tok, 2]
        sums_send(tok, 1)

    def finish(tok):
        sums[tok, 1].wait_recv()
        gtot = (gy[tok] + gy_in[tok, 0] + gy_in[tok, 1] + gy_in[tok, 2]) * (1.0 / D)
        rows = pl.ds(pl.multiple_of(tok * 256 + r * 16, 16), 16)
        inv = pick(mi[1], tok * 16 + r)
        normed = (noisy[rows, :] - pick(mi[0], tok * 16 + r)) * inv
        v = inv * (pick(gtot[0], r) + normed * pick(gtot[1], r))
        t1 = v.astype(BF16)
        t2 = (v - t1.astype(F32)).astype(BF16)
        t3 = (v - t1.astype(F32) - t2.astype(F32)).astype(BF16)
        one = ohs[:, 0:16]
        rest4 = (dot_nn(one, t1) + dot_nn(one, t2) + dot_nn(one, t3))[0:4]
        tot = rs[tok, r].astype(F32)
        parts[tok].wait_recv()
        for k in range(1, 16):
            tot = tot + rr[tok, k].astype(F32)
        for q in range(4):
            lo = q * 768
            fin = (tot[q * 4 : q * 4 + 4] * gain_ref[:, lo : lo + 768] - rest4[:, lo : lo + 768]) / cnt4
            la_own[tok, :, lo : lo + 768] = fin.astype(BF16)
        for s in (4, 3, 5, 2, 6, 1, 7):
            late[tok].send(la_own.at[tok], outb_hbm.at[2 * z + tok], z_peer(s))

    back_part(0)
    cp_bk[0].start()
    hidden(0)
    spread(0)
    sums_y(0)
    back_part(1)
    cp_bk[1].start()
    hidden(1)
    finish(0)
    spread(1)
    sums_y(1)
    ea.wait_recv()
    ld_ea.wait()
    old = [cp for cp in live if cp is not parts[1] and cp is not sums[1, 1]]
    for cp in old:
        if cp is not late[0]:
            cp.wait_send()
    finish(1)
    ld_la = pltpu.make_async_copy(la_own, outb_hbm.at[pl.ds(2 * z, 2)], load_sem.at[5])
    ld_la.start()
    for tok in range(2):
        late[tok].wait_recv()
    for cp in (parts[1], sums[1, 1], late[0], late[1]):
        cp.wait_send()
    ld_la.wait()


def body(images, gain, up_weight, down_weight, cotangent, seeds, assign):
    vm, dma = pltpu.VMEM, pltpu.SemaphoreType.DMA
    anyspace = pl.BlockSpec(memory_space=pl.ANY)
    early, late = pl.pallas_call(
        kernel,
        out_shape=[jax.ShapeDtypeStruct((16, 4, 3072), F32), jax.ShapeDtypeStruct((16, 4, 3072), BF16)],
        in_specs=[
            anyspace,
            pl.BlockSpec(memory_space=pltpu.VMEM),
            anyspace,
            anyspace,
            anyspace,
            pl.BlockSpec(memory_space=pltpu.SMEM),
            pl.BlockSpec(memory_space=pltpu.SMEM),
        ],
        out_specs=[anyspace, anyspace],
        scratch_shapes=[
            vm((3072, 768), BF16),
            vm((768, 3072), BF16),
            vm((2, 4, 3072), BF16),
            vm((16, 1536), F32),
            vm((2, 4, 4, 16, 768), BF16),
            vm((8, 2, 2, 3072), BF16),
            vm((8, 8, 128), I32),
            vm((32, 3072), F32),
            vm((2, 2, 4, 4, 16, 1536), BF16),
            vm((2, 2, 512, 256), BF16),
            vm((16, 3072), I32),
            vm((512, 3072), F32),
            vm((528, 3072), BF16),
            vm((2, 2, 128, 768), F32),
            vm((2, 128, 768), F32),
            vm((16, 768), F32),
            vm((16, 768), F32),
            vm((2, 128, 768), F32),
            vm((2, 2, 128, 768), F32),
            vm((2, 128, 768), F32),
            vm((2, 16, 128), F32),
            vm((2, 16, 128), F32),
            vm((2, 16, 128), F32),
            vm((2, 2, 16, 128), F32),
            vm((2, 2, 16, 128), F32),
            vm((128, 128), F32),
            vm((2, 96, 128), BF16),
            vm((2, 128, 768), BF16),
            vm((2, 2, 2, 32, 768), BF16),
            vm((2, 4, 64, 768), F32),
            vm((2, 16, 16, 768), BF16),
            vm((2, 16, 16, 768), BF16),
            vm((2, 2, 16, 128), F32),
            vm((2, 3, 2, 16, 128), F32),
            vm((2, 2, 16, 128), F32),
            vm((2, 3, 2, 16, 128), F32),
            vm((16, 128), BF16),
            vm((2, 4, 3072), F32),
            vm((2, 4, 3072), BF16),
            dma((6,)),
            dma((2,)), dma((2,)),
            dma((2,)), dma((2,)),
            dma((2, 2)), dma((2, 2)),
            dma((5, 2)), dma((5, 2)),
            dma((2,)), dma((2,)),
            dma((2, 2)), dma((2, 2)),
            dma((1,)), dma((1,)),
            dma((2,)), dma((2,)),
        ],
        compiler_params=pltpu.CompilerParams(
            collective_id=0, has_side_effects=True, vmem_limit_bytes=56 * 1024 * 1024
        ),
        cost_estimate=pl.CostEstimate(flops=8 * 10**9, bytes_accessed=12 * 10**6, transcendentals=200000),
    )(images, gain.reshape(1, -1), up_weight, down_weight, cotangent, seeds, assign.reshape(-1))
    return early + late.astype(F32)


def solution(mesh):
    placed = (
        P("row", None, "col"),
        P("col"),
        P("col", "row"),
        P("row", "col"),
        P("row", "noise", "col"),
        P("noise"),
        P(),
    )
    return jax.shard_map(
        body, mesh=mesh, in_specs=placed, out_specs=P("row", None, "col"), check_vma=False
    )
```

```python
import math

import jax
import jax.numpy as jnp
from jax import lax
from jax.experimental import pallas as pl
from jax.experimental.pallas import tpu as pltpu
from jax.sharding import PartitionSpec as P

D = 6144
noise_scale = 0.6
gelu_coef = 0.044715
root_term = math.sqrt(2.0 / math.pi)
MESH = pl.DeviceIdType.MESH
F32 = jnp.float32
BF16 = jnp.bfloat16
I32 = jnp.int32


def gelu_slope(preact):
    inner = root_term * (preact + gelu_coef * preact * preact * preact)
    tanh_val = jnp.tanh(inner)
    return 0.5 * (1.0 + tanh_val) + 0.5 * preact * (1.0 - tanh_val * tanh_val) * root_term * (
        1.0 + 3.0 * gelu_coef * preact * preact
    )


def dot_nt(a, b):
    return lax.dot_general(a, b, (((1,), (1,)), ((), ())), preferred_element_type=F32)


def dot_nn(a, b):
    return lax.dot_general(a, b, (((1,), (0,)), ((), ())), preferred_element_type=F32)


class Copies:
    def __init__(self, live, ssem, rsem, whole, dev):
        self.live, self.ssem, self.rsem = live, ssem, rsem
        self.whole = lambda: pltpu.make_async_remote_copy(
            src_ref=whole, dst_ref=whole, send_sem=ssem, recv_sem=rsem, device_id=dev, device_id_type=MESH
        )

    def send(self, src, dst, dev):
        if self not in self.live:
            self.live.append(self)
        pltpu.make_async_remote_copy(
            src_ref=src, dst_ref=dst, send_sem=self.ssem, recv_sem=self.rsem, device_id=dev, device_id_type=MESH
        ).start()

    def wait_recv(self):
        self.whole().wait_recv()

    def wait_send(self):
        self.whole().wait_send()


class Copy(Copies):
    def __init__(self, live, src, dst, ssem, rsem, dev):
        super().__init__(live, ssem, rsem, dst, dev)
        self.start = lambda: self.send(src, dst, dev)


def wrap(i, n):
    return lax.rem(i + n, n)


def kernel(
    img_hbm, gain_ref, up_hbm, dn_hbm, cot_hbm, seeds_ref, assign_ref, outa_hbm, outb_hbm,
    up_v, dn_v, img_own, pk16, imgg, rc, seedg, pk32, cg, onehot, base, noisy, scl,
    pre, pre_in, ugp, ug_in, slope, bk, bk_in, stat, stat_in, mi, gst, gst_in, wt, wm, hgb, wall,
    o_s, rs, rr, gx, gx_in, gy, gy_in, ohs, ea_own, la_own,
    load_sem, z_send, z_recv, i_send, i_recv, c_send, c_recv, k_send, k_recv,
    r_send, r_recv, g_send, g_recv, e_send, e_recv, l_send, l_recv,
):
    z = lax.axis_index("noise")
    r = lax.axis_index("row")
    c = lax.axis_index("col")
    y, x = r // 4, lax.rem(r, 4)
    p1 = (x, y)
    p2 = (y, x)

    def row_peer(ab, phase, step):
        along_x = (ab == 0) == (phase == 1)
        if along_x:
            return {"row": y * 4 + wrap(x + step, 4)}
        return {"row": wrap(y + step, 4) * 4 + x}

    def z_peer(step):
        return {"noise": wrap(z + step, 8)}

    other = {"col": 1 - c}

    live = []

    def rcopy(src, dst, ssem, rsem, dev):
        return Copy(live, src, dst, ssem, rsem, dev)

    ld_img = pltpu.make_async_copy(img_hbm.at[pl.ds(2 * z, 2)], img_own, load_sem.at[0])
    ld_img.start()
    ld_cot = pltpu.make_async_copy(cot_hbm.at[pl.ds(2 * z, 2)], rc.at[z], load_sem.at[1])
    ld_cot.start()
    ld_up = pltpu.make_async_copy(up_hbm, up_v, load_sem.at[2])
    ld_up.start()
    ld_dn = pltpu.make_async_copy(dn_hbm, dn_v, load_sem.at[3])
    ld_dn.start()

    barrier = pltpu.get_barrier_semaphore()
    for dev in (
        [z_peer(s) for s in range(1, 8)]
        + [{"row": wrap(y + k // 4, 4) * 4 + wrap(x + k % 4, 4)} for k in range(1, 16)]
        + [other]
    ):
        pl.semaphore_signal(barrier, inc=1, device_id=dev, device_id_type=MESH)

    seedg[z] = jnp.where(
        lax.broadcasted_iota(I32, (8, 128), 0) == 0, seeds_ref[0], seeds_ref[1]
    )
    ld_img.wait()
    for tok in range(2):
        v = img_own[tok].astype(F32)
        for q in range(4):
            ab, half = q // 2, q % 2
            pk16[half * 8 + tok * 4 : half * 8 + tok * 4 + 4, ab * 768 : (ab + 1) * 768] = v[
                :, q * 768 : (q + 1) * 768
            ]
    for ab in range(2):
        imgg[ab, p2[ab], p1[ab]] = pk16[:, ab * 768 : ab * 768 + 768].astype(BF16)
    pl.semaphore_wait(barrier, 23)

    z_order = (1, 7, 2, 6, 3, 5, 4)
    z_seed = Copies(live, z_send.at[0], z_recv.at[0], seedg.at[pl.ds(0, 7)], z_peer(1))
    z_cot = Copies(live, z_send.at[1], z_recv.at[1], rc.at[pl.ds(0, 7)], z_peer(1))
    for s in z_order:
        z_cot.send(cot_hbm.at[pl.ds(2 * wrap(z + s, 8), 2)], rc.at[z], z_peer(s))

    class Gather:
        def __init__(self, buf, ssem, rsem):
            three = pl.ds(0, 3)
            whole = (buf.at[pl.ds(0, 2), 0, three], buf.at[pl.ds(0, 2), three])
            self.buf = buf
            self.copies = [
                Copies(live, ssem.at[n], rsem.at[n], whole[n], row_peer(0, n + 1, 1)) for n in range(2)
            ]

        def start(self, phase):
            for step in (1, 3, 2):
                for ab in range(2):
                    own = self.buf.at[ab, p2[ab], p1[ab]] if phase == 1 else self.buf.at[ab, p2[ab]]
                    self.copies[phase - 1].send(own, own, row_peer(ab, phase, step))

        def wait(self, phase):
            self.copies[phase - 1].wait_recv()

    img_g = Gather(imgg, i_send, i_recv)
    cot_g = [Gather(cg.at[j], c_send.at[j], c_recv.at[j]) for j in range(2)]

    img_g.start(1)
    for s in z_order:
        z_seed.send(seedg.at[z], seedg.at[z], z_peer(s))

    sub16 = lax.broadcasted_iota(I32, (16, 128), 0)
    lane = lax.broadcasted_iota(I32, (16, 128), 1)
    a16 = jnp.zeros((16, 128), I32)
    for s in range(16):
        a16 = jnp.where(sub16 == s, assign_ref[s], a16)
    cnt = [jnp.float32(0.0)] * 4
    for s in range(16):
        for i in range(4):
            cnt[i] = cnt[i] + jnp.where(assign_ref[s] == i, 1.0, 0.0)
    counts = jnp.ones((16, 128), F32)
    for i in range(4):
        counts = jnp.where(sub16 == i, cnt[i], counts)
    cnt4 = counts[0:4, 0:1]
    sel = jnp.zeros((16, 128), F32)
    for s in range(16):
        sel = jnp.where((lane == s) & (sub16 == assign_ref[s]), 1.0, sel)
    ohs[...] = sel.astype(BF16)

    def swap(b):
        return lax.rem(b, 4) * 4 + b // 4

    a16w = jnp.concatenate([a16, a16], axis=1)
    col16 = lax.broadcasted_iota(I32, (16, 256), 1)
    for tok in range(2):
        for ab in range(2):
            for half in range(2):

                def fill(b, _, tok=tok, ab=ab, half=half):
                    blk = b if ab == 0 else swap(b)
                    target = a16w + (blk * 16 + half * 8 + tok * 4)
                    onehot[ab, half, pl.ds(pl.multiple_of(tok * 256 + b * 16, 16), 16), :] = jnp.where(
                        col16 == target, 1.0, 0.0
                    ).astype(BF16)
                    return 0

                lax.fori_loop(0, 16, fill, 0)

    img_g.wait(1)
    img_g.start(2)

    g0 = gain_ref[...]
    g_hi = g0.astype(BF16)
    g_mid = (g0 - g_hi.astype(F32)).astype(BF16)
    g_lo = (g0 - g_hi.astype(F32) - g_mid.astype(F32)).astype(BF16)
    sub_g = lax.broadcasted_iota(I32, (16, 3072), 0)
    scl[512:528, :] = jnp.where(
        sub_g == 0,
        g_hi.astype(F32),
        jnp.where(sub_g == 1, g_mid.astype(F32), jnp.where(sub_g == 2, g_lo.astype(F32), 0.0)),
    ).astype(BF16)
    z_seed.wait_recv()
    for k in range(8):
        for e in range(2):
            s = 2 * k + e
            pos = lax.broadcasted_iota(I32, (1, 3072), 1)
            row = seedg[k, e : e + 1, 0:1] * 1013904223
            base[s : s + 1, :] = (pos + c * 3072) * 1664525 + row

    def field_blocks(tok):
        def four(k, _):
            for u in range(4):
                b = k * 4 + u
                mixed = base[...] + (b * 16 + z * 2 + tok) * D * 1664525
                mixed = mixed ^ (mixed >> 13)
                mixed = mixed * 1274126177
                mixed = mixed ^ (mixed >> 16)
                field = (mixed & 65535).astype(F32) - 32767.5
                noisy[pl.ds(pl.multiple_of(tok * 256 + b * 16, 16), 16), :] = field * (noise_scale / 18918.0)
            return 0

        lax.fori_loop(0, 4, four, 0)

    def pack_cot(tok):
        for k in range(8):
            pk32[tok * 16 + 2 * k : tok * 16 + 2 * k + 2, :] = rc[k, tok].astype(F32)
        for ab in range(2):
            cg[tok, ab, p2[ab], p1[ab]] = pk32[tok * 16 : tok * 16 + 16, ab * 1536 : ab * 1536 + 1536].astype(BF16)
        cot_g[tok].start(1)

    def pump(k):
        cot_g[k].wait(1)
        cot_g[k].start(2)

    z_cot.wait_recv()
    ld_cot.wait()
    pack_cot(0)
    pack_cot(1)
    for tok in range(2):
        early = dot_nn(ohs[:, 0:16], pk32[tok * 16 : tok * 16 + 16, :].astype(BF16))
        ea_own[tok] = early[0:4] / cnt4
    ld_ea = pltpu.make_async_copy(ea_own, outa_hbm.at[pl.ds(2 * z, 2)], load_sem.at[4])
    ld_ea.start()
    ea = Copies(live, e_send.at[0], e_recv.at[0], outa_hbm.at[pl.ds(0, 14)], z_peer(1))
    for s in z_order:
        ea.send(ea_own, outa_hbm.at[pl.ds(2 * z, 2)], z_peer(s))
    field_blocks(0)
    field_blocks(1)
    pump(0)
    img_g.wait(2)
    for ab in range(2):
        for half in range(2):
            lo = ab * 1536 + half * 768
            noisy[:, lo : lo + 768] = noisy[:, lo : lo + 768] + dot_nn(
                onehot[ab, half], imgg[ab].reshape(256, 768)
            )
    pump(1)

    def stat_blocks(k, carry):
        tot, m2 = carry
        for u in range(4):
            n = k * 4 + u
            v = noisy[pl.ds(pl.multiple_of(n * 16, 16), 16), :]
            s1 = jnp.sum(v, axis=1, keepdims=True)
            dev = v - s1 * (1.0 / 3072.0)
            s2 = jnp.sum(dev * dev, axis=1, keepdims=True)
            hit = lane == n
            tot, m2 = jnp.where(hit, s1, tot), jnp.where(hit, s2, m2)
        return tot, m2

    carry = lax.fori_loop(0, 8, stat_blocks, (jnp.zeros((16, 128), F32), jnp.zeros((16, 128), F32)))
    stat[0], stat[1] = carry
    cp_stat = rcopy(stat, stat_in, k_send.at[1, 1], k_recv.at[1, 1], other)
    cp_stat.start()
    cp_stat.wait_recv()
    mean_a, mean_b = stat[0] * (1.0 / 3072.0), stat_in[0] * (1.0 / 3072.0)
    gap = mean_a - mean_b
    var = (stat[1] + stat_in[1] + gap * gap * 1536.0) * (1.0 / D)
    mi[0] = (mean_a + mean_b) * 0.5
    mi[1] = lax.rsqrt(var + 1e-06)

    def pick(arr, idx):
        return jnp.sum(jnp.where(lane == idx, arr, 0.0), axis=1, keepdims=True)

    def norm_blocks(k4, _):
        for u in range(4):
            k = k4 * 4 + u
            rows = pl.ds(pl.multiple_of(k * 16, 16), 16)
            normed = (noisy[rows, :] - pick(mi[0], k)) * pick(mi[1], k)
            scl[rows, :] = (normed * gain_ref[...]).astype(BF16)
        return 0

    lax.fori_loop(0, 8, norm_blocks, 0)
    ld_up.wait()
    ld_dn.wait()

    def pre_cols(n):
        res = dot_nn(scl[...], up_v[:, n * 256 : (n + 1) * 256])
        for tok in range(2):
            for h in range(2):
                lo = tok * 256 + h * 128
                pre[tok, h, :, n * 256 : (n + 1) * 256] = res[lo : lo + 128]
        ugp[:, n * 256 : (n + 1) * 256] = res[512:528]

    pre_cols(0)
    pre_cols(1)
    pre_cols(2)
    cp_pre = [
        rcopy(pre.at[tok, 1 - c], pre_in.at[tok], k_send.at[0, tok], k_recv.at[0, tok], other) for tok in range(2)
    ]
    for cp in cp_pre:
        cp.start()
    cp_ug = rcopy(ugp, ug_in, k_send.at[1, 0], k_recv.at[1, 0], other)
    cp_ug.start()

    def back_part(tok):
        cot_g[tok].wait(2)
        for ab in range(2):
            lo = ab * 1536
            res = dot_nt(cg[tok, ab].reshape(256, 1536), dn_v[:, lo : lo + 1536])
            for b in range(16):
                at = b if ab == 0 else (b % 4) * 4 + b // 4
                part = res[at * 16 : at * 16 + 16]
                h, lb = b // 8, (b % 8) * 16
                if ab == 0:
                    bk[tok, h, lb : lb + 16] = part
                else:
                    bk[tok, h, lb : lb + 16] = bk[tok, h, lb : lb + 16] + part

    cp_bk = [rcopy(bk.at[tok, 1 - c], bk_in.at[tok], k_send.at[2, tok], k_recv.at[2, tok], other) for tok in range(2)]
    cp_gst = [rcopy(gst.at[tok], gst_in.at[tok], k_send.at[3, tok], k_recv.at[3, tok], other) for tok in range(2)]
    cp_w = [
        rcopy(wall.at[tok, c], wall.at[tok, c], k_send.at[4, tok], k_recv.at[4, tok], other) for tok in range(2)
    ]

    sums = {
        (tok, axis): Copies(
            live, g_send.at[tok, axis], g_recv.at[tok, axis], (gx_in, gy_in)[axis].at[tok], row_peer(0, axis + 1, 1)
        )
        for tok in range(2)
        for axis in range(2)
    }

    def sums_send(tok, axis):
        src, dst = ((gx, gx_in), (gy, gy_in))[axis]
        for step in (1, 3, 2):
            sums[tok, axis].send(src.at[tok], dst.at[tok, step - 1], row_peer(0, axis + 1, step))

    far = sorted(range(1, 16), key=lambda k: min(k // 4, 4 - k // 4) + min(k % 4, 4 - k % 4))
    parts = [
        Copies(live, r_send.at[tok], r_recv.at[tok], rr.at[tok, pl.ds(1, 15)], row_peer(0, 1, 1)) for tok in range(2)
    ]
    late = [
        Copies(live, l_send.at[tok], l_recv.at[tok], outb_hbm.at[pl.ds(0, 7)], z_peer(1)) for tok in range(2)
    ]

    for tok in range(2):
        cp_pre[tok].wait_recv()
    cp_ug.wait_recv()
    for tok in range(2):

        def slope_block(k, _, tok=tok):
            for u in range(2):
                rows = pl.ds(pl.multiple_of(k * 32 + u * 16, 16), 16)
                p = pre[tok, c, rows, :] + pre_in[tok, rows, :]
                pre_in[tok, rows, :] = p
                slope[tok, rows, :] = gelu_slope(p)
            return 0

        lax.fori_loop(0, 4, slope_block, 0)
    ug = (ugp[0:1] + ugp[1:2] + ugp[2:3]) + (ug_in[0:1] + ug_in[1:2] + ug_in[2:3])
    for tok in range(2):
        for b in range(8):
            inv = pick(mi[1], tok * 16 + c * 8 + b)
            wt[b * 16 : b * 16 + 16, :] = jnp.where(lane == b * 4 + a16, inv, 0.0)
        full = wt[...].T[0:32]
        hi = full.astype(BF16)
        mid = (full - hi.astype(F32)).astype(BF16)
        lo = (full - hi.astype(F32) - mid.astype(F32)).astype(BF16)
        wm[tok, 0:32] = hi
        wm[tok, 32:64] = mid
        wm[tok, 64:96] = lo

    def hidden(tok):
        cp_bk[tok].wait_recv()

        def hidden_blocks(k, carry):
            gs, gd = carry
            for u in range(4):
                b = k * 4 + u
                rows = pl.ds(pl.multiple_of(b * 16, 16), 16)
                hg = ((bk[tok, c, rows, :] + bk_in[tok, rows, :]) * slope[tok, rows, :]).astype(BF16)
                hgb[tok, rows, :] = hg
                hf = hg.astype(F32)
                s1 = jnp.sum(hf * ug, axis=1, keepdims=True)
                s2 = jnp.sum(hf * pre_in[tok, rows, :], axis=1, keepdims=True)
                hit = lane == c * 8 + b
                gs, gd = jnp.where(hit, s1, gs), jnp.where(hit, s2, gd)
            return gs, gd

        zero = jnp.zeros((16, 128), F32)
        gst[tok, 0], gst[tok, 1] = lax.fori_loop(0, 2, hidden_blocks, (zero, zero))
        wsum = dot_nn(wm[tok], hgb[tok])
        wsum = wsum[0:32] + wsum[32:64] + wsum[64:96]
        w_hi = wsum.astype(BF16)
        wall[tok, c, 0] = w_hi
        wall[tok, c, 1] = (wsum - w_hi.astype(F32)).astype(BF16)
        cp_w[tok].start()
        cp_gst[tok].start()

    def spread(tok):
        cp_w[tok].wait_recv()
        cp_gst[tok].wait_recv()
        gx[tok] = gst[tok] + gst_in[tok]
        sums_send(tok, 0)
        for q in range(4):
            o = dot_nt(wall[tok].reshape(128, 768), up_v[q * 768 : (q + 1) * 768, :])
            o_s[tok, q, 0:32] = o[0:32] + o[32:64]
            o_s[tok, q, 32:64] = o[64:96] + o[96:128]

        def pack(k, _):
            rows = pl.ds(pl.multiple_of(k * 8, 8), 8)
            v = [o_s[tok, q, rows, :] for q in range(4)]
            for u in range(2):
                rs[tok, k * 2 + u] = jnp.concatenate([w[u * 4 : u * 4 + 4] for w in v], axis=0).astype(BF16)
            return 0

        lax.fori_loop(0, 8, pack, 0)
        for k in far:
            peer = wrap(y + k // 4, 4) * 4 + wrap(x + k % 4, 4)
            parts[tok].send(rs.at[tok, peer], rr.at[tok, k], {"row": peer})

    def sums_y(tok):
        sums[tok, 0].wait_recv()
        gy[tok] = gx[tok] + gx_in[tok, 0] + gx_in[tok, 1] + gx_in[tok, 2]
        sums_send(tok, 1)

    def finish(tok):
        sums[tok, 1].wait_recv()
        gtot = (gy[tok] + gy_in[tok, 0] + gy_in[tok, 1] + gy_in[tok, 2]) * (1.0 / D)
        rows = pl.ds(pl.multiple_of(tok * 256 + r * 16, 16), 16)
        inv = pick(mi[1], tok * 16 + r)
        normed = (noisy[rows, :] - pick(mi[0], tok * 16 + r)) * inv
        v = inv * (pick(gtot[0], r) + normed * pick(gtot[1], r))
        t1 = v.astype(BF16)
        t2 = (v - t1.astype(F32)).astype(BF16)
        t3 = (v - t1.astype(F32) - t2.astype(F32)).astype(BF16)
        one = ohs[:, 0:16]
        rest4 = (dot_nn(one, t1) + dot_nn(one, t2) + dot_nn(one, t3))[0:4]
        tot = rs[tok, r].astype(F32)
        parts[tok].wait_recv()
        for k in range(1, 16):
            tot = tot + rr[tok, k].astype(F32)
        for q in range(4):
            lo = q * 768
            fin = (tot[q * 4 : q * 4 + 4] * gain_ref[:, lo : lo + 768] - rest4[:, lo : lo + 768]) / cnt4
            la_own[tok, :, lo : lo + 768] = fin.astype(BF16)
        for s in (4, 3, 5, 2, 6, 1, 7):
            late[tok].send(la_own.at[tok], outb_hbm.at[2 * z + tok], z_peer(s))

    back_part(0)
    cp_bk[0].start()
    hidden(0)
    spread(0)
    sums_y(0)
    back_part(1)
    cp_bk[1].start()
    hidden(1)
    spread(1)
    sums_y(1)
    finish(0)
    ea.wait_recv()
    ld_ea.wait()
    old = [cp for cp in live if cp is not parts[1] and cp is not sums[1, 1]]
    for cp in old:
        if cp is not late[0]:
            cp.wait_send()
    finish(1)
    ld_la = pltpu.make_async_copy(la_own, outb_hbm.at[pl.ds(2 * z, 2)], load_sem.at[5])
    ld_la.start()
    for tok in range(2):
        late[tok].wait_recv()
    for cp in (parts[1], sums[1, 1], late[0], late[1]):
        cp.wait_send()
    ld_la.wait()


def body(images, gain, up_weight, down_weight, cotangent, seeds, assign):
    vm, dma = pltpu.VMEM, pltpu.SemaphoreType.DMA
    anyspace = pl.BlockSpec(memory_space=pl.ANY)
    early, late = pl.pallas_call(
        kernel,
        out_shape=[jax.ShapeDtypeStruct((16, 4, 3072), F32), jax.ShapeDtypeStruct((16, 4, 3072), BF16)],
        in_specs=[
            anyspace,
            pl.BlockSpec(memory_space=pltpu.VMEM),
            anyspace,
            anyspace,
            anyspace,
            pl.BlockSpec(memory_space=pltpu.SMEM),
            pl.BlockSpec(memory_space=pltpu.SMEM),
        ],
        out_specs=[anyspace, anyspace],
        scratch_shapes=[
            vm((3072, 768), BF16),
            vm((768, 3072), BF16),
            vm((2, 4, 3072), BF16),
            vm((16, 1536), F32),
            vm((2, 4, 4, 16, 768), BF16),
            vm((8, 2, 2, 3072), BF16),
            vm((8, 8, 128), I32),
            vm((32, 3072), F32),
            vm((2, 2, 4, 4, 16, 1536), BF16),
            vm((2, 2, 512, 256), BF16),
            vm((16, 3072), I32),
            vm((512, 3072), F32),
            vm((528, 3072), BF16),
            vm((2, 2, 128, 768), F32),
            vm((2, 128, 768), F32),
            vm((16, 768), F32),
            vm((16, 768), F32),
            vm((2, 128, 768), F32),
            vm((2, 2, 128, 768), F32),
            vm((2, 128, 768), F32),
            vm((2, 16, 128), F32),
            vm((2, 16, 128), F32),
            vm((2, 16, 128), F32),
            vm((2, 2, 16, 128), F32),
            vm((2, 2, 16, 128), F32),
            vm((128, 128), F32),
            vm((2, 96, 128), BF16),
            vm((2, 128, 768), BF16),
            vm((2, 2, 2, 32, 768), BF16),
            vm((2, 4, 64, 768), F32),
            vm((2, 16, 16, 768), BF16),
            vm((2, 16, 16, 768), BF16),
            vm((2, 2, 16, 128), F32),
            vm((2, 3, 2, 16, 128), F32),
            vm((2, 2, 16, 128), F32),
            vm((2, 3, 2, 16, 128), F32),
            vm((16, 128), BF16),
            vm((2, 4, 3072), F32),
            vm((2, 4, 3072), BF16),
            dma((6,)),
            dma((2,)), dma((2,)),
            dma((2,)), dma((2,)),
            dma((2, 2)), dma((2, 2)),
            dma((5, 2)), dma((5, 2)),
            dma((2,)), dma((2,)),
            dma((2, 2)), dma((2, 2)),
            dma((1,)), dma((1,)),
            dma((2,)), dma((2,)),
        ],
        compiler_params=pltpu.CompilerParams(
            collective_id=0, has_side_effects=True, vmem_limit_bytes=56 * 1024 * 1024
        ),
        cost_estimate=pl.CostEstimate(flops=8 * 10**9, bytes_accessed=12 * 10**6, transcendentals=200000),
    )(images, gain.reshape(1, -1), up_weight, down_weight, cotangent, seeds, assign.reshape(-1))
    return early + late.astype(F32)


def solution(mesh):
    placed = (
        P("row", None, "col"),
        P("col"),
        P("col", "row"),
        P("row", "col"),
        P("row", "noise", "col"),
        P("noise"),
        P(),
    )
    return jax.shard_map(
        body, mesh=mesh, in_specs=placed, out_specs=P("row", None, "col"), check_vma=False
    )
```

```python
import math

import jax
import jax.numpy as jnp
from jax import lax
from jax.experimental import pallas as pl
from jax.experimental.pallas import tpu as pltpu
from jax.sharding import PartitionSpec as P

D = 6144
noise_scale = 0.6
gelu_coef = 0.044715
root_term = math.sqrt(2.0 / math.pi)
MESH = pl.DeviceIdType.MESH
F32 = jnp.float32
BF16 = jnp.bfloat16
I32 = jnp.int32


def gelu_slope(preact):
    inner = root_term * (preact + gelu_coef * preact * preact * preact)
    tanh_val = jnp.tanh(inner)
    return 0.5 * (1.0 + tanh_val) + 0.5 * preact * (1.0 - tanh_val * tanh_val) * root_term * (
        1.0 + 3.0 * gelu_coef * preact * preact
    )


def dot_nt(a, b):
    return lax.dot_general(a, b, (((1,), (1,)), ((), ())), preferred_element_type=F32)


def dot_nn(a, b):
    return lax.dot_general(a, b, (((1,), (0,)), ((), ())), preferred_element_type=F32)


class Copies:
    def __init__(self, live, ssem, rsem, whole, dev):
        self.live, self.ssem, self.rsem = live, ssem, rsem
        self.whole = lambda: pltpu.make_async_remote_copy(
            src_ref=whole, dst_ref=whole, send_sem=ssem, recv_sem=rsem, device_id=dev, device_id_type=MESH
        )

    def send(self, src, dst, dev):
        if self not in self.live:
            self.live.append(self)
        pltpu.make_async_remote_copy(
            src_ref=src, dst_ref=dst, send_sem=self.ssem, recv_sem=self.rsem, device_id=dev, device_id_type=MESH
        ).start()

    def wait_recv(self):
        self.whole().wait_recv()

    def wait_send(self):
        self.whole().wait_send()


class Copy(Copies):
    def __init__(self, live, src, dst, ssem, rsem, dev):
        super().__init__(live, ssem, rsem, dst, dev)
        self.start = lambda: self.send(src, dst, dev)


def wrap(i, n):
    return lax.rem(i + n, n)


def kernel(
    img_hbm, gain_ref, up_hbm, dn_hbm, cot_hbm, seeds_ref, assign_ref, outa_hbm, outb_hbm,
    up_v, dn_v, img_own, pk16, imgg, rc, seedg, pk32, cg, onehot, base, noisy, scl,
    pre, pre_in, ugp, ug_in, slope, bk, bk_in, stat, stat_in, mi, gst, gst_in, wt, wm, hgb, wall,
    o_s, rs, rr, gx, gx_in, gy, gy_in, ohs, ea_own, la_own,
    load_sem, z_send, z_recv, i_send, i_recv, c_send, c_recv, k_send, k_recv,
    r_send, r_recv, g_send, g_recv, e_send, e_recv, l_send, l_recv,
):
    z = lax.axis_index("noise")
    r = lax.axis_index("row")
    c = lax.axis_index("col")
    y, x = r // 4, lax.rem(r, 4)
    p1 = (x, y)
    p2 = (y, x)

    def row_peer(ab, phase, step):
        along_x = (ab == 0) == (phase == 1)
        if along_x:
            return {"row": y * 4 + wrap(x + step, 4)}
        return {"row": wrap(y + step, 4) * 4 + x}

    def z_peer(step):
        return {"noise": wrap(z + step, 8)}

    other = {"col": 1 - c}

    live = []

    def rcopy(src, dst, ssem, rsem, dev):
        return Copy(live, src, dst, ssem, rsem, dev)

    ld_img = pltpu.make_async_copy(img_hbm.at[pl.ds(2 * z, 2)], img_own, load_sem.at[0])
    ld_img.start()
    ld_cot = pltpu.make_async_copy(cot_hbm.at[pl.ds(2 * z, 2)], rc.at[z], load_sem.at[1])
    ld_cot.start()
    ld_up = pltpu.make_async_copy(up_hbm, up_v, load_sem.at[2])
    ld_up.start()
    ld_dn = pltpu.make_async_copy(dn_hbm, dn_v, load_sem.at[3])
    ld_dn.start()

    barrier = pltpu.get_barrier_semaphore()
    for dev in (
        [z_peer(s) for s in range(1, 8)]
        + [{"row": wrap(y + k // 4, 4) * 4 + wrap(x + k % 4, 4)} for k in range(1, 16)]
        + [other]
    ):
        pl.semaphore_signal(barrier, inc=1, device_id=dev, device_id_type=MESH)

    seedg[z] = jnp.where(
        lax.broadcasted_iota(I32, (8, 128), 0) == 0, seeds_ref[0], seeds_ref[1]
    )
    ld_img.wait()
    for tok in range(2):
        v = img_own[tok].astype(F32)
        for q in range(4):
            ab, half = q // 2, q % 2
            pk16[half * 8 + tok * 4 : half * 8 + tok * 4 + 4, ab * 768 : (ab + 1) * 768] = v[
                :, q * 768 : (q + 1) * 768
            ]
    for ab in range(2):
        imgg[ab, p2[ab], p1[ab]] = pk16[:, ab * 768 : ab * 768 + 768].astype(BF16)
    pl.semaphore_wait(barrier, 23)

    z_order = (1, 7, 2, 6, 3, 5, 4)
    z_seed = Copies(live, z_send.at[0], z_recv.at[0], seedg.at[pl.ds(0, 7)], z_peer(1))
    z_cot = Copies(live, z_send.at[1], z_recv.at[1], rc.at[pl.ds(0, 7)], z_peer(1))
    for s in z_order:
        z_cot.send(cot_hbm.at[pl.ds(2 * wrap(z + s, 8), 2)], rc.at[z], z_peer(s))

    class Gather:
        def __init__(self, buf, ssem, rsem):
            three = pl.ds(0, 3)
            whole = (buf.at[pl.ds(0, 2), 0, three], buf.at[pl.ds(0, 2), three])
            self.buf = buf
            self.copies = [
                Copies(live, ssem.at[n], rsem.at[n], whole[n], row_peer(0, n + 1, 1)) for n in range(2)
            ]

        def start(self, phase):
            for step in (1, 3, 2):
                for ab in range(2):
                    own = self.buf.at[ab, p2[ab], p1[ab]] if phase == 1 else self.buf.at[ab, p2[ab]]
                    self.copies[phase - 1].send(own, own, row_peer(ab, phase, step))

        def wait(self, phase):
            self.copies[phase - 1].wait_recv()

    img_g = Gather(imgg, i_send, i_recv)
    cot_g = [Gather(cg.at[j], c_send.at[j], c_recv.at[j]) for j in range(2)]

    img_g.start(1)
    for s in z_order:
        z_seed.send(seedg.at[z], seedg.at[z], z_peer(s))

    sub16 = lax.broadcasted_iota(I32, (16, 128), 0)
    lane = lax.broadcasted_iota(I32, (16, 128), 1)
    a16 = jnp.zeros((16, 128), I32)
    for s in range(16):
        a16 = jnp.where(sub16 == s, assign_ref[s], a16)
    cnt = [jnp.float32(0.0)] * 4
    for s in range(16):
        for i in range(4):
            cnt[i] = cnt[i] + jnp.where(assign_ref[s] == i, 1.0, 0.0)
    counts = jnp.ones((16, 128), F32)
    for i in range(4):
        counts = jnp.where(sub16 == i, cnt[i], counts)
    cnt4 = counts[0:4, 0:1]
    sel = jnp.zeros((16, 128), F32)
    for s in range(16):
        sel = jnp.where((lane == s) & (sub16 == assign_ref[s]), 1.0, sel)
    ohs[...] = sel.astype(BF16)

    def swap(b):
        return lax.rem(b, 4) * 4 + b // 4

    a16w = jnp.concatenate([a16, a16], axis=1)
    col16 = lax.broadcasted_iota(I32, (16, 256), 1)
    for tok in range(2):
        for ab in range(2):
            for half in range(2):

                def fill(b, _, tok=tok, ab=ab, half=half):
                    blk = b if ab == 0 else swap(b)
                    target = a16w + (blk * 16 + half * 8 + tok * 4)
                    onehot[ab, half, pl.ds(pl.multiple_of(tok * 256 + b * 16, 16), 16), :] = jnp.where(
                        col16 == target, 1.0, 0.0
                    ).astype(BF16)
                    return 0

                lax.fori_loop(0, 16, fill, 0)

    img_g.wait(1)
    img_g.start(2)

    g0 = gain_ref[...]
    g_hi = g0.astype(BF16)
    g_mid = (g0 - g_hi.astype(F32)).astype(BF16)
    g_lo = (g0 - g_hi.astype(F32) - g_mid.astype(F32)).astype(BF16)
    sub_g = lax.broadcasted_iota(I32, (16, 3072), 0)
    scl[512:528, :] = jnp.where(
        sub_g == 0,
        g_hi.astype(F32),
        jnp.where(sub_g == 1, g_mid.astype(F32), jnp.where(sub_g == 2, g_lo.astype(F32), 0.0)),
    ).astype(BF16)
    z_seed.wait_recv()
    for k in range(8):
        for e in range(2):
            s = 2 * k + e
            pos = lax.broadcasted_iota(I32, (1, 3072), 1)
            row = seedg[k, e : e + 1, 0:1] * 1013904223
            base[s : s + 1, :] = (pos + c * 3072) * 1664525 + row

    def field_blocks(tok):
        def four(k, _):
            for u in range(4):
                b = k * 4 + u
                mixed = base[...] + (b * 16 + z * 2 + tok) * D * 1664525
                mixed = mixed ^ (mixed >> 13)
                mixed = mixed * 1274126177
                mixed = mixed ^ (mixed >> 16)
                field = (mixed & 65535).astype(F32) - 32767.5
                noisy[pl.ds(pl.multiple_of(tok * 256 + b * 16, 16), 16), :] = field * (noise_scale / 18918.0)
            return 0

        lax.fori_loop(0, 4, four, 0)

    def pack_cot(tok):
        for k in range(8):
            pk32[tok * 16 + 2 * k : tok * 16 + 2 * k + 2, :] = rc[k, tok].astype(F32)
        for ab in range(2):
            cg[tok, ab, p2[ab], p1[ab]] = pk32[tok * 16 : tok * 16 + 16, ab * 1536 : ab * 1536 + 1536].astype(BF16)
        cot_g[tok].start(1)

    def pump(k):
        cot_g[k].wait(1)
        cot_g[k].start(2)

    z_cot.wait_recv()
    ld_cot.wait()
    pack_cot(0)
    pack_cot(1)
    for tok in range(2):
        early = dot_nn(ohs[:, 0:16], pk32[tok * 16 : tok * 16 + 16, :].astype(BF16))
        ea_own[tok] = early[0:4] / cnt4
    ld_ea = pltpu.make_async_copy(ea_own, outa_hbm.at[pl.ds(2 * z, 2)], load_sem.at[4])
    ld_ea.start()
    ea = Copies(live, e_send.at[0], e_recv.at[0], outa_hbm.at[pl.ds(0, 14)], z_peer(1))
    for s in z_order:
        ea.send(ea_own, outa_hbm.at[pl.ds(2 * z, 2)], z_peer(s))
    field_blocks(0)
    field_blocks(1)
    pump(0)
    img_g.wait(2)
    for ab in range(2):
        for half in range(2):
            lo = ab * 1536 + half * 768
            noisy[:, lo : lo + 768] = noisy[:, lo : lo + 768] + dot_nn(
                onehot[ab, half], imgg[ab].reshape(256, 768)
            )
    def stat_blocks(k, carry):
        tot, m2 = carry
        for u in range(4):
            n = k * 4 + u
            v = noisy[pl.ds(pl.multiple_of(n * 16, 16), 16), :]
            s1 = jnp.sum(v, axis=1, keepdims=True)
            dev = v - s1 * (1.0 / 3072.0)
            s2 = jnp.sum(dev * dev, axis=1, keepdims=True)
            hit = lane == n
            tot, m2 = jnp.where(hit, s1, tot), jnp.where(hit, s2, m2)
        return tot, m2

    carry = lax.fori_loop(0, 8, stat_blocks, (jnp.zeros((16, 128), F32), jnp.zeros((16, 128), F32)))
    stat[0], stat[1] = carry
    cp_stat = rcopy(stat, stat_in, k_send.at[1, 1], k_recv.at[1, 1], other)
    cp_stat.start()
    cp_stat.wait_recv()
    mean_a, mean_b = stat[0] * (1.0 / 3072.0), stat_in[0] * (1.0 / 3072.0)
    gap = mean_a - mean_b
    var = (stat[1] + stat_in[1] + gap * gap * 1536.0) * (1.0 / D)
    mi[0] = (mean_a + mean_b) * 0.5
    mi[1] = lax.rsqrt(var + 1e-06)

    def pick(arr, idx):
        return jnp.sum(jnp.where(lane == idx, arr, 0.0), axis=1, keepdims=True)

    def norm_blocks(k4, _):
        for u in range(4):
            k = k4 * 4 + u
            rows = pl.ds(pl.multiple_of(k * 16, 16), 16)
            normed = (noisy[rows, :] - pick(mi[0], k)) * pick(mi[1], k)
            scl[rows, :] = (normed * gain_ref[...]).astype(BF16)
        return 0

    lax.fori_loop(0, 8, norm_blocks, 0)
    ld_up.wait()
    ld_dn.wait()

    def pre_cols(n):
        res = dot_nn(scl[...], up_v[:, n * 256 : (n + 1) * 256])
        for tok in range(2):
            for h in range(2):
                lo = tok * 256 + h * 128
                pre[tok, h, :, n * 256 : (n + 1) * 256] = res[lo : lo + 128]
        ugp[:, n * 256 : (n + 1) * 256] = res[512:528]

    pump(1)
    pre_cols(0)
    pre_cols(1)
    pre_cols(2)
    cp_pre = [
        rcopy(pre.at[tok, 1 - c], pre_in.at[tok], k_send.at[0, tok], k_recv.at[0, tok], other) for tok in range(2)
    ]
    for cp in cp_pre:
        cp.start()
    cp_ug = rcopy(ugp, ug_in, k_send.at[1, 0], k_recv.at[1, 0], other)
    cp_ug.start()

    def back_part(tok):
        cot_g[tok].wait(2)
        for ab in range(2):
            lo = ab * 1536
            res = dot_nt(cg[tok, ab].reshape(256, 1536), dn_v[:, lo : lo + 1536])
            for b in range(16):
                at = b if ab == 0 else (b % 4) * 4 + b // 4
                part = res[at * 16 : at * 16 + 16]
                h, lb = b // 8, (b % 8) * 16
                if ab == 0:
                    bk[tok, h, lb : lb + 16] = part
                else:
                    bk[tok, h, lb : lb + 16] = bk[tok, h, lb : lb + 16] + part

    cp_bk = [rcopy(bk.at[tok, 1 - c], bk_in.at[tok], k_send.at[2, tok], k_recv.at[2, tok], other) for tok in range(2)]
    cp_gst = [rcopy(gst.at[tok], gst_in.at[tok], k_send.at[3, tok], k_recv.at[3, tok], other) for tok in range(2)]
    cp_w = [
        rcopy(wall.at[tok, c], wall.at[tok, c], k_send.at[4, tok], k_recv.at[4, tok], other) for tok in range(2)
    ]

    sums = {
        (tok, axis): Copies(
            live, g_send.at[tok, axis], g_recv.at[tok, axis], (gx_in, gy_in)[axis].at[tok], row_peer(0, axis + 1, 1)
        )
        for tok in range(2)
        for axis in range(2)
    }

    def sums_send(tok, axis):
        src, dst = ((gx, gx_in), (gy, gy_in))[axis]
        for step in (1, 3, 2):
            sums[tok, axis].send(src.at[tok], dst.at[tok, step - 1], row_peer(0, axis + 1, step))

    far = sorted(range(1, 16), key=lambda k: min(k // 4, 4 - k // 4) + min(k % 4, 4 - k % 4))
    parts = [
        Copies(live, r_send.at[tok], r_recv.at[tok], rr.at[tok, pl.ds(1, 15)], row_peer(0, 1, 1)) for tok in range(2)
    ]
    late = [
        Copies(live, l_send.at[tok], l_recv.at[tok], outb_hbm.at[pl.ds(0, 7)], z_peer(1)) for tok in range(2)
    ]

    for tok in range(2):
        cp_pre[tok].wait_recv()
    cp_ug.wait_recv()
    for tok in range(2):

        def slope_block(k, _, tok=tok):
            for u in range(2):
                rows = pl.ds(pl.multiple_of(k * 32 + u * 16, 16), 16)
                p = pre[tok, c, rows, :] + pre_in[tok, rows, :]
                pre_in[tok, rows, :] = p
                slope[tok, rows, :] = gelu_slope(p)
            return 0

        lax.fori_loop(0, 4, slope_block, 0)
    ug = (ugp[0:1] + ugp[1:2] + ugp[2:3]) + (ug_in[0:1] + ug_in[1:2] + ug_in[2:3])
    for tok in range(2):
        for b in range(8):
            inv = pick(mi[1], tok * 16 + c * 8 + b)
            wt[b * 16 : b * 16 + 16, :] = jnp.where(lane == b * 4 + a16, inv, 0.0)
        full = wt[...].T[0:32]
        hi = full.astype(BF16)
        mid = (full - hi.astype(F32)).astype(BF16)
        lo = (full - hi.astype(F32) - mid.astype(F32)).astype(BF16)
        wm[tok, 0:32] = hi
        wm[tok, 32:64] = mid
        wm[tok, 64:96] = lo

    def hidden(tok):
        cp_bk[tok].wait_recv()

        def hidden_blocks(k, carry):
            gs, gd = carry
            for u in range(4):
                b = k * 4 + u
                rows = pl.ds(pl.multiple_of(b * 16, 16), 16)
                hg = ((bk[tok, c, rows, :] + bk_in[tok, rows, :]) * slope[tok, rows, :]).astype(BF16)
                hgb[tok, rows, :] = hg
                hf = hg.astype(F32)
                s1 = jnp.sum(hf * ug, axis=1, keepdims=True)
                s2 = jnp.sum(hf * pre_in[tok, rows, :], axis=1, keepdims=True)
                hit = lane == c * 8 + b
                gs, gd = jnp.where(hit, s1, gs), jnp.where(hit, s2, gd)
            return gs, gd

        zero = jnp.zeros((16, 128), F32)
        gst[tok, 0], gst[tok, 1] = lax.fori_loop(0, 2, hidden_blocks, (zero, zero))
        wsum = dot_nn(wm[tok], hgb[tok])
        wsum = wsum[0:32] + wsum[32:64] + wsum[64:96]
        w_hi = wsum.astype(BF16)
        wall[tok, c, 0] = w_hi
        wall[tok, c, 1] = (wsum - w_hi.astype(F32)).astype(BF16)
        cp_w[tok].start()
        cp_gst[tok].start()

    def spread(tok):
        cp_w[tok].wait_recv()
        cp_gst[tok].wait_recv()
        gx[tok] = gst[tok] + gst_in[tok]
        sums_send(tok, 0)
        for q in range(4):
            o = dot_nt(wall[tok].reshape(128, 768), up_v[q * 768 : (q + 1) * 768, :])
            o_s[tok, q, 0:32] = o[0:32] + o[32:64]
            o_s[tok, q, 32:64] = o[64:96] + o[96:128]

        def pack(k, _):
            rows = pl.ds(pl.multiple_of(k * 8, 8), 8)
            v = [o_s[tok, q, rows, :] for q in range(4)]
            for u in range(2):
                rs[tok, k * 2 + u] = jnp.concatenate([w[u * 4 : u * 4 + 4] for w in v], axis=0).astype(BF16)
            return 0

        lax.fori_loop(0, 8, pack, 0)
        for k in far:
            peer = wrap(y + k // 4, 4) * 4 + wrap(x + k % 4, 4)
            parts[tok].send(rs.at[tok, peer], rr.at[tok, k], {"row": peer})

    def sums_y(tok):
        sums[tok, 0].wait_recv()
        gy[tok] = gx[tok] + gx_in[tok, 0] + gx_in[tok, 1] + gx_in[tok, 2]
        sums_send(tok, 1)

    def finish(tok):
        sums[tok, 1].wait_recv()
        gtot = (gy[tok] + gy_in[tok, 0] + gy_in[tok, 1] + gy_in[tok, 2]) * (1.0 / D)
        rows = pl.ds(pl.multiple_of(tok * 256 + r * 16, 16), 16)
        inv = pick(mi[1], tok * 16 + r)
        normed = (noisy[rows, :] - pick(mi[0], tok * 16 + r)) * inv
        v = inv * (pick(gtot[0], r) + normed * pick(gtot[1], r))
        t1 = v.astype(BF16)
        t2 = (v - t1.astype(F32)).astype(BF16)
        t3 = (v - t1.astype(F32) - t2.astype(F32)).astype(BF16)
        one = ohs[:, 0:16]
        rest4 = (dot_nn(one, t1) + dot_nn(one, t2) + dot_nn(one, t3))[0:4]
        tot = rs[tok, r].astype(F32)
        parts[tok].wait_recv()
        for k in range(1, 16):
            tot = tot + rr[tok, k].astype(F32)
        for q in range(4):
            lo = q * 768
            fin = (tot[q * 4 : q * 4 + 4] * gain_ref[:, lo : lo + 768] - rest4[:, lo : lo + 768]) / cnt4
            la_own[tok, :, lo : lo + 768] = fin.astype(BF16)
        for s in (4, 3, 5, 2, 6, 1, 7):
            late[tok].send(la_own.at[tok], outb_hbm.at[2 * z + tok], z_peer(s))

    back_part(0)
    cp_bk[0].start()
    hidden(0)
    spread(0)
    sums_y(0)
    back_part(1)
    cp_bk[1].start()
    hidden(1)
    spread(1)
    sums_y(1)
    finish(0)
    ea.wait_recv()
    ld_ea.wait()
    old = [cp for cp in live if cp is not parts[1] and cp is not sums[1, 1]]
    for cp in old:
        if cp is not late[0]:
            cp.wait_send()
    finish(1)
    ld_la = pltpu.make_async_copy(la_own, outb_hbm.at[pl.ds(2 * z, 2)], load_sem.at[5])
    ld_la.start()
    for tok in range(2):
        late[tok].wait_recv()
    for cp in (parts[1], sums[1, 1], late[0], late[1]):
        cp.wait_send()
    ld_la.wait()


def body(images, gain, up_weight, down_weight, cotangent, seeds, assign):
    vm, dma = pltpu.VMEM, pltpu.SemaphoreType.DMA
    anyspace = pl.BlockSpec(memory_space=pl.ANY)
    early, late = pl.pallas_call(
        kernel,
        out_shape=[jax.ShapeDtypeStruct((16, 4, 3072), F32), jax.ShapeDtypeStruct((16, 4, 3072), BF16)],
        in_specs=[
            anyspace,
            pl.BlockSpec(memory_space=pltpu.VMEM),
            anyspace,
            anyspace,
            anyspace,
            pl.BlockSpec(memory_space=pltpu.SMEM),
            pl.BlockSpec(memory_space=pltpu.SMEM),
        ],
        out_specs=[anyspace, anyspace],
        scratch_shapes=[
            vm((3072, 768), BF16),
            vm((768, 3072), BF16),
            vm((2, 4, 3072), BF16),
            vm((16, 1536), F32),
            vm((2, 4, 4, 16, 768), BF16),
            vm((8, 2, 2, 3072), BF16),
            vm((8, 8, 128), I32),
            vm((32, 3072), F32),
            vm((2, 2, 4, 4, 16, 1536), BF16),
            vm((2, 2, 512, 256), BF16),
            vm((16, 3072), I32),
            vm((512, 3072), F32),
            vm((528, 3072), BF16),
            vm((2, 2, 128, 768), F32),
            vm((2, 128, 768), F32),
            vm((16, 768), F32),
            vm((16, 768), F32),
            vm((2, 128, 768), F32),
            vm((2, 2, 128, 768), F32),
            vm((2, 128, 768), F32),
            vm((2, 16, 128), F32),
            vm((2, 16, 128), F32),
            vm((2, 16, 128), F32),
            vm((2, 2, 16, 128), F32),
            vm((2, 2, 16, 128), F32),
            vm((128, 128), F32),
            vm((2, 96, 128), BF16),
            vm((2, 128, 768), BF16),
            vm((2, 2, 2, 32, 768), BF16),
            vm((2, 4, 64, 768), F32),
            vm((2, 16, 16, 768), BF16),
            vm((2, 16, 16, 768), BF16),
            vm((2, 2, 16, 128), F32),
            vm((2, 3, 2, 16, 128), F32),
            vm((2, 2, 16, 128), F32),
            vm((2, 3, 2, 16, 128), F32),
            vm((16, 128), BF16),
            vm((2, 4, 3072), F32),
            vm((2, 4, 3072), BF16),
            dma((6,)),
            dma((2,)), dma((2,)),
            dma((2,)), dma((2,)),
            dma((2, 2)), dma((2, 2)),
            dma((5, 2)), dma((5, 2)),
            dma((2,)), dma((2,)),
            dma((2, 2)), dma((2, 2)),
            dma((1,)), dma((1,)),
            dma((2,)), dma((2,)),
        ],
        compiler_params=pltpu.CompilerParams(
            collective_id=0, has_side_effects=True, vmem_limit_bytes=56 * 1024 * 1024
        ),
        cost_estimate=pl.CostEstimate(flops=8 * 10**9, bytes_accessed=12 * 10**6, transcendentals=200000),
    )(images, gain.reshape(1, -1), up_weight, down_weight, cotangent, seeds, assign.reshape(-1))
    return early + late.astype(F32)


def solution(mesh):
    placed = (
        P("row", None, "col"),
        P("col"),
        P("col", "row"),
        P("row", "col"),
        P("row", "noise", "col"),
        P("noise"),
        P(),
    )
    return jax.shard_map(
        body, mesh=mesh, in_specs=placed, out_specs=P("row", None, "col"), check_vma=False
    )
```
